128 devices in a mesh: outer: 4 (over z), inner: 32 (over x, y, core).
Axes of the slice: x: 4, y: 4, z: 4, core: 2. Of those that a mesh axis runs over, the one named last changes fastest.
Arguments:
- query_rows: bfloat16 [16384, 2048], P(('outer', 'inner')), may hold values from -7.1 to 7.1
- key_rows: bfloat16 [16384, 2048], P(('outer', 'inner')), may hold values from -7.1 to 7.1
- value_rows: bfloat16 [16384, 2048], P(('outer', 'inner')), may hold values from -6 to 6
- sample_of: int32 [16384], P(('outer', 'inner')), may hold values from 0 to 7, never falling along the last dimension, each value on 1 to 4096 neighbouring positions
- cotangent: bfloat16 [16384, 2048], P(('outer', 'inner')), may hold values from -6 to 6
Outputs:
- attended: bfloat16 [16384, 2048], P(('outer', 'inner'))
- grad_query: bfloat16 [16384, 2048], P(('outer', 'inner'))
- grad_key: bfloat16 [16384, 2048], P(('outer', 'inner'))
- grad_value: bfloat16 [16384, 2048], P(('outer', 'inner'))
The draws below stay inside these ranges and needn't reach their ends.
Inputs may be any that keep to these rules, and one draw needn't show every extreme that they name: `sample_of`: sample ids never fall along the tokens; each of the 8 samples holds 1 to 4096 tokens, and one holds exactly 4096.
All inputs are finite; a program needn't handle non-finite values.
Results may differ from the reference program's by a relative error of at most 0.012.
The reference program's roundings to bfloat16 on the way (of `weights` and `grad_score`) count: a program that leaves them out, or rounds other values in their place, can miss the bound.
Values may be sent and summed in bfloat16 or wider, within the bound.
A program may use at most 64 MiB of HBM per device.

```python
import math
import jax
import jax.numpy as jnp
import numpy as np
from jax import lax

H = 32
HD = 64
GROUP_TOK = 4096
TOKENS = 16384
L_MAX = 4096
SAMPLES = 8


def draw_query_rows(key, part):
    key = jax.random.fold_in(key, 5)
    drawn_rows = jax.random.truncated_normal(key, -4.0, 4.0, (TOKENS, H * HD), jnp.float32)
    return drawn_rows.astype(jnp.bfloat16)


def draw_key_rows(key, part):
    key = jax.random.fold_in(key, 9)
    drawn_rows = jax.random.truncated_normal(key, -4.0, 4.0, (TOKENS, H * HD), jnp.float32)
    return drawn_rows.astype(jnp.bfloat16)


def block_scale(own_key, extent, cuts, smallest, top_value):
    loudness, own = 1.0, jax.random.fold_in(own_key, 6)
    for position, shards_of in cuts:
        heights = jnp.exp(jax.random.uniform(jax.random.fold_in(own, position), (shards_of,), jnp.float32, smallest / len(cuts), top_value / len(cuts)))
        loudness = loudness * jnp.repeat(heights, extent[position] // shards_of).reshape([-1 if axis == position else 1 for axis in range(len(extent))])
    return loudness


def profile(number_of, total, limit, skew):
    weights = [(1 << 20) // math.isqrt(standing ** skew) + 1 for standing in range(2, number_of + 1)]
    rest, holding = total - limit - (number_of - 1), [1] * (number_of - 1)
    while rest > 0:
        free = [i for i in range(number_of - 1) if holding[i] < limit]
        whole, remaining = sum([weights[i] for i in free]), rest
        for i in free:
            extra = min(limit - holding[i], max(1, remaining * weights[i] // whole), rest)
            holding[i] = holding[i] + extra
            rest = rest - extra
    return np.array([limit] + holding)


def ragged(rng, number_of, total, bound, skew):
    if number_of == 2:
        one = jax.random.randint(rng, (), max(1, total - bound), min(bound, total - 1) + 1)
        return jnp.stack([one, total - one])
    sizes = jnp.asarray(profile(number_of, total, bound, skew), jnp.int32)
    couples = (number_of - 1) // 2
    source_of, sink = sizes[1:1 + 2 * couples:2], sizes[2:2 + 2 * couples:2]
    slack = jnp.minimum(source_of - 1, bound - sink)
    passed = jax.random.randint(jax.random.fold_in(rng, 1), (couples,), 0, 1 << 20) % (slack + 1)
    sizes = sizes.at[1:1 + 2 * couples:2].set(source_of - passed).at[2:2 + 2 * couples:2].set(sink + passed)
    return sizes[jax.random.permutation(jax.random.fold_in(rng, 2), number_of)]


def scatter_about(key, extent, spread, bound, pieces=(), kind=jnp.bfloat16):
    array = jax.random.normal(key, extent, jnp.float32) * spread
    if len(pieces) > 0:
        array = block_scale(key, extent, pieces, -0.22, 0.18) * array
    return jnp.clip(array, min=-bound, max=bound).astype(kind)


def setup_inputs(seed: int = 0) -> dict:
    key_of = jax.random.split(jax.random.key(seed), 6)
    query_rows = draw_query_rows(jax.random.fold_in(key_of[5], 71), 0)
    key_rows = draw_key_rows(jax.random.fold_in(key_of[5], 71), 0)
    value_rows = scatter_about(key_of[2], (TOKENS, H * HD), 1.0, 6.0, ((0, 128),))
    sample_of = jnp.searchsorted(jnp.cumsum(ragged(key_of[3], SAMPLES, TOKENS, L_MAX, 2)), jnp.arange(TOKENS), side="right").astype(jnp.int32)
    cotangent = scatter_about(key_of[4], (TOKENS, H * HD), 1.0, 6.0, ((0, 128),))
    return {"query_rows": query_rows, "key_rows": key_rows, "value_rows": value_rows, "sample_of": sample_of, "cotangent": cotangent}


masked_fill = -1e+30

def padded_rows(values, margin):
    widths = [(margin, margin)] + [(0, 0)] * (values.ndim - 1)
    return jnp.pad(values, widths)

def pair_scores(query_tile, key_tile, factor):
    return jnp.einsum('qhd,khd->hqk', query_tile.astype(jnp.float32), key_tile.astype(jnp.float32)) * factor

def reference(query_rows, key_rows, value_rows, sample_of, cotangent):
    factor = 1.0 / math.sqrt(HD)
    tile_rows = math.gcd(TOKENS, 256)
    margin = L_MAX
    window = tile_rows + 2 * margin
    tile_count = TOKENS // tile_rows
    query_heads = query_rows.reshape(TOKENS, H, HD)
    key_heads = key_rows.reshape(TOKENS, H, HD)
    value_heads = value_rows.reshape(TOKENS, H, HD)
    cot_heads = cotangent.reshape(TOKENS, H, HD)
    query_pad = padded_rows(query_heads, margin)
    key_pad = padded_rows(key_heads, margin)
    value_pad = padded_rows(value_heads, margin)
    cot_pad = padded_rows(cot_heads, margin)
    edge_ids = jnp.full((margin,), -1, jnp.int32)
    ids_pad = jnp.concatenate([edge_ids, sample_of.astype(jnp.int32), edge_ids])
    tile_list = jnp.arange(tile_count, dtype=jnp.int32)

    def window_of(values, row_start):
        return lax.dynamic_slice_in_dim(values, row_start, window, 0)

    def tile_of(values, row_start):
        return lax.dynamic_slice_in_dim(values, row_start, tile_rows, 0)

    def forward_tile(tile_idx):
        row_start = (tile_idx * tile_rows).astype(jnp.int32)
        query_tile = tile_of(query_heads, row_start)
        own_ids = tile_of(sample_of, row_start)
        key_win = window_of(key_pad, row_start)
        value_win = window_of(value_pad, row_start)
        ids_win = window_of(ids_pad, row_start)
        allowed = (own_ids[:, None] == ids_win[None, :])[None]
        scores = pair_scores(query_tile, key_win, factor)
        row_max = lax.optimization_barrier(jnp.max(jnp.where(allowed, scores, masked_fill), axis=2))
        row_sum = lax.optimization_barrier(jnp.sum(jnp.where(allowed, jnp.exp(scores - row_max[:, :, None]), 0.0), axis=2))
        log_norm = row_max + jnp.log(row_sum)
        weights = jnp.where(allowed, jnp.exp(scores - log_norm[:, :, None]), 0.0).astype(jnp.bfloat16)
        mixed_rows = jnp.einsum('hqk,khd->qhd', weights.astype(jnp.float32), value_win.astype(jnp.float32))
        return (mixed_rows.astype(jnp.bfloat16), log_norm)
    mixed_tiles, log_tiles = lax.map(forward_tile, tile_list)
    attended_heads = mixed_tiles.reshape(TOKENS, H, HD)
    log_rows = jnp.transpose(log_tiles, (0, 2, 1)).reshape(TOKENS, H)
    row_dot = lax.optimization_barrier(jnp.sum(cot_heads.astype(jnp.float32) * attended_heads.astype(jnp.float32), axis=2))
    log_pad = padded_rows(log_rows, margin)
    dot_pad = padded_rows(row_dot, margin)

    def query_grad_tile(tile_idx):
        row_start = (tile_idx * tile_rows).astype(jnp.int32)
        query_tile = tile_of(query_heads, row_start)
        cot_tile = tile_of(cot_heads, row_start)
        own_ids = tile_of(sample_of, row_start)
        log_tile = tile_of(log_rows, row_start)
        dot_tile = tile_of(row_dot, row_start)
        key_win = window_of(key_pad, row_start)
        value_win = window_of(value_pad, row_start)
        ids_win = window_of(ids_pad, row_start)
        allowed = (own_ids[:, None] == ids_win[None, :])[None]
        scores = pair_scores(query_tile, key_win, factor)
        weights_exact = jnp.where(allowed, jnp.exp(scores - log_tile.T[:, :, None]), 0.0)
        grad_prob = jnp.einsum('qhd,khd->hqk', cot_tile.astype(jnp.float32), value_win.astype(jnp.float32))
        grad_score = (weights_exact * (grad_prob - dot_tile.T[:, :, None])).astype(jnp.bfloat16)
        query_sum = jnp.einsum('hqk,khd->qhd', grad_score.astype(jnp.float32), key_win.astype(jnp.float32)) * factor
        return query_sum.astype(jnp.bfloat16)

    def key_grad_tile(tile_idx):
        row_start = (tile_idx * tile_rows).astype(jnp.int32)
        key_tile = tile_of(key_heads, row_start)
        value_tile = tile_of(value_heads, row_start)
        own_ids = tile_of(sample_of, row_start)
        query_win = window_of(query_pad, row_start)
        cot_win = window_of(cot_pad, row_start)
        ids_win = window_of(ids_pad, row_start)
        log_win = window_of(log_pad, row_start)
        dot_win = window_of(dot_pad, row_start)
        allowed = (ids_win[:, None] == own_ids[None, :])[None]
        scores = pair_scores(query_win, key_tile, factor)
        weights_exact = jnp.where(allowed, jnp.exp(scores - log_win.T[:, :, None]), 0.0)
        grad_prob = jnp.einsum('qhd,khd->hqk', cot_win.astype(jnp.float32), value_tile.astype(jnp.float32))
        grad_score = (weights_exact * (grad_prob - dot_win.T[:, :, None])).astype(jnp.bfloat16)
        weights_round = weights_exact.astype(jnp.bfloat16)
        key_groups = (row_start + jnp.arange(tile_rows, dtype=jnp.int32)) // GROUP_TOK
        groups = (row_start - margin + jnp.arange(window, dtype=jnp.int32)) // GROUP_TOK
        key_sum = jnp.zeros((tile_rows, H, HD), jnp.float32)
        value_sum = jnp.zeros((tile_rows, H, HD), jnp.float32)
        for offset in (-1, 0, 1):
            chosen = (groups[:, None] == key_groups[None, :] + offset).astype(jnp.float32)[None]
            part_key = jnp.einsum('hqk,qhd->khd', grad_score.astype(jnp.float32) * chosen, query_win.astype(jnp.float32)) * factor
            part_value = jnp.einsum('hqk,qhd->khd', weights_round.astype(jnp.float32) * chosen, cot_win.astype(jnp.float32))
            part_key = lax.optimization_barrier(part_key.astype(jnp.bfloat16))
            part_value = lax.optimization_barrier(part_value.astype(jnp.bfloat16))
            key_sum = key_sum + part_key.astype(jnp.float32)
            value_sum = value_sum + part_value.astype(jnp.float32)
        return (key_sum.astype(jnp.bfloat16), value_sum.astype(jnp.bfloat16))
    query_grads = lax.map(query_grad_tile, tile_list).reshape(TOKENS, H * HD)
    key_grads, value_grads = lax.map(key_grad_tile, tile_list)
    attended = attended_heads.reshape(TOKENS, H * HD)
    return (attended, query_grads, key_grads.reshape(TOKENS, H * HD), value_grads.reshape(TOKENS, H * HD))
```

```python
import functools, math
import jax, jax.numpy as jnp
from jax import lax
from jax.sharding import PartitionSpec as P
from jax.experimental import pallas as pl
from jax.experimental.pallas import tpu as pltpu

H, HD, SAMPLES = 32, 64, 8
TQ, TK, ALIGN = 256, 512, 128
PENALTY = -float(2**20)


def attention_kernel(starts, counts, qc_ref, kv_ref, qid_ref, kid_ref, mix_ref, dkv_ref,
                     kaug, kvx, kvT, acc, pbuf, mbuf):
    rows, ext = qc_ref.shape[0], kv_ref.shape[0]
    factor = 1.0 / math.sqrt(HD)
    log2_factor = factor * math.log2(math.e)
    f32, bf16 = jnp.float32, jnp.bfloat16

    def one_hot(ids_row, width):
        sample = lax.broadcasted_iota(jnp.int32, (SAMPLES, width), 0)
        return sample == jnp.broadcast_to(ids_row, (SAMPLES, width))

    def prepare(block, _):
        at = pl.multiple_of(block * TK, TK)
        here = pl.ds(at, TK)
        tile = kv_ref[here, :]
        turned = tile.T
        kvx[here, :] = tile
        kvT[:, here] = turned
        penalty = jnp.where(one_hot(kid_ref[:, here], TK), 0.0, PENALTY)
        penalty = jnp.concatenate([penalty, jnp.zeros((HD - SAMPLES, TK), f32)], axis=0)
        kaug[here, :] = jnp.concatenate([turned[:HD], penalty.astype(bf16)], axis=0).T
        acc[here, :] = jnp.zeros((TK, 2 * HD), f32)
        return 0

    lax.fori_loop(0, ext // TK, prepare, 0)
    pad = pl.ds(ext, TK)
    lane = lax.broadcasted_iota(jnp.int32, (TK, 2 * HD), 1)
    kvx[pad, :] = jnp.zeros((TK, 2 * HD), bf16)
    kvT[:, pad] = jnp.zeros((2 * HD, TK), bf16)
    kaug[pad, :] = jnp.where((lane >= HD) & (lane < HD + SAMPLES), PENALTY, 0.0).astype(bf16)
    acc[pad, :] = jnp.zeros((TK, 2 * HD), f32)

    def query_tile(tile, _):
        q_at = pl.multiple_of(tile * TQ, TQ)
        mine = pl.ds(q_at, TQ)
        qc = qc_ref[mine, :]
        qcT = qc.T
        qT, cT = qcT[:HD], qcT[HD:]
        hot = jnp.where(one_hot(qid_ref[:, mine], TQ), 1.0, 0.0)
        hot = jnp.concatenate([hot, jnp.zeros((HD - SAMPLES, TQ), f32)], axis=0).astype(bf16)
        q_side = jnp.concatenate([qT, hot], axis=0)
        c_side = jnp.concatenate([jnp.zeros_like(cT), cT], axis=0)
        lanes = lax.broadcasted_iota(jnp.int32, qc.shape, 1)
        q_only = jnp.where(lanes < HD, qc, jnp.zeros_like(qc))
        c_only = jnp.where(lanes < HD, jnp.zeros_like(qc), qc)
        cq = jnp.concatenate([c_only, q_only], axis=0)
        first = starts[tile]
        count = counts[tile]

        def key_rows(step):
            return pl.ds(pl.multiple_of(first + step * TK, ALIGN), TK)

        def slot(step):
            return pl.ds(pl.multiple_of(step * TK, TK), TK)

        def score_step(step, state):
            top, total = state
            scores = jnp.dot(kaug[key_rows(step), :], q_side, preferred_element_type=f32) * log2_factor
            new_top = jnp.maximum(top, jnp.max(scores, axis=0, keepdims=True))
            terms = jnp.exp2(scores - new_top)
            pbuf[slot(step), :] = terms
            mbuf[step] = new_top
            return new_top, total * jnp.exp2(top - new_top) + jnp.sum(terms, axis=0, keepdims=True)

        top, total = lax.fori_loop(
            0, count, score_step, (jnp.full((1, TQ), -1e30, f32), jnp.zeros((1, TQ), f32))
        )
        scale = 1.0 / total

        def value_step(step, summed):
            weights = pbuf[slot(step), :] * (jnp.exp2(mbuf[step] - top) * scale)
            return summed + jnp.dot(
                kvT[HD:, key_rows(step)], weights.astype(bf16), preferred_element_type=f32
            )

        mixed = lax.fori_loop(0, count, value_step, jnp.zeros((HD, TQ), f32)).astype(bf16)
        row_dot = jnp.sum(cT.astype(f32) * mixed.astype(f32), axis=0, keepdims=True)

        def grad_step(step, summed):
            keys = key_rows(step)
            weights = pbuf[slot(step), :] * (jnp.exp2(mbuf[step] - top) * scale)
            grad_prob = jnp.dot(kvx[keys, :], c_side, preferred_element_type=f32)
            grad_score = (weights * (grad_prob - row_dot)).astype(bf16)
            pair = jnp.concatenate([weights.astype(bf16), grad_score], axis=1)
            acc[keys, :] += jnp.dot(pair, cq, preferred_element_type=f32)
            return summed + jnp.dot(kvT[:HD, keys], grad_score, preferred_element_type=f32)

        grad_query = lax.fori_loop(0, count, grad_step, jnp.zeros((HD, TQ), f32)) * factor
        mix_ref[mine, :] = jnp.concatenate([mixed, grad_query.astype(bf16)], axis=0).T
        return 0

    lax.fori_loop(0, rows // TQ, query_tile, 0)

    def finish(block, _):
        here = pl.ds(pl.multiple_of(block * TK, TK), TK)
        grads = acc[here, :]
        dkv_ref[here, :] = jnp.where(lane < HD, grads * factor, grads).astype(bf16)
        return 0

    lax.fori_loop(0, ext // TK, finish, 0)


def attention(starts, counts, qc, kv, qid, kid):
    rows, ext = qc.shape[0], kv.shape[0]
    vmem = pl.BlockSpec(memory_space=pltpu.VMEM)
    smem = pl.BlockSpec(memory_space=pltpu.SMEM)
    most = 2 * rows + TQ + TK + ALIGN
    return pl.pallas_call(
        attention_kernel,
        out_shape=(jax.ShapeDtypeStruct((rows, 2 * HD), jnp.bfloat16),
                   jax.ShapeDtypeStruct((ext, 2 * HD), jnp.bfloat16)),
        in_specs=[smem, smem, vmem, vmem, vmem, vmem],
        out_specs=(vmem, vmem),
        scratch_shapes=[
            pltpu.VMEM((ext + TK, 2 * HD), jnp.bfloat16),
            pltpu.VMEM((ext + TK, 2 * HD), jnp.bfloat16),
            pltpu.VMEM((2 * HD, ext + TK), jnp.bfloat16),
            pltpu.VMEM((ext + TK, 2 * HD), jnp.float32),
            pltpu.VMEM(((most + TK - 1) // TK * TK, TQ), jnp.float32),
            pltpu.VMEM(((most + TK - 1) // TK, 1, TQ), jnp.float32),
        ],
        compiler_params=pltpu.CompilerParams(vmem_limit_bytes=56 * 2**20),
        name="attention",
    )(starts, counts, qc, kv, qid, kid)


def on_device(query_rows, key_rows, value_rows, sample_of, cotangent):
    inner = lax.axis_size("inner")
    outer = lax.axis_size("outer")
    tok = query_rows.shape[0]
    rows = tok * inner
    all_ids = lax.all_gather(sample_of, ("outer", "inner"), axis=0, tiled=True)
    group = lax.axis_index("outer")
    padded = jnp.concatenate([jnp.full((rows,), -1, jnp.int32), all_ids, jnp.full((rows,), SAMPLES, jnp.int32)])
    row_ids = lax.dynamic_slice_in_dim(all_ids, group * rows, rows, 0)
    ext_ids = lax.dynamic_slice_in_dim(padded, group * rows, 3 * rows, 0)
    tiles = row_ids.reshape(rows // TQ, TQ)
    low = jnp.sum((ext_ids[None, :] < tiles[:, :1]).astype(jnp.int32), axis=1)
    high = jnp.sum((ext_ids[None, :] <= tiles[:, -1:]).astype(jnp.int32), axis=1)
    starts = low // ALIGN * ALIGN
    counts = (high - starts + TK - 1) // TK

    def pair(a, b):
        a = a.reshape(tok, inner, HD)
        b = b.reshape(tok, inner, HD)
        both = jnp.concatenate([a, b], axis=2)
        return lax.all_to_all(both, "inner", split_axis=1, concat_axis=0, tiled=True).reshape(rows, 2 * HD)

    kv = pair(key_rows, value_rows)
    up = [(i, i + 1) for i in range(outer - 1)]
    down = [(j, i) for i, j in up]
    before = lax.ppermute(kv, "outer", up)
    after = lax.ppermute(kv, "outer", down)
    qc = pair(query_rows, cotangent)
    kv_ext = jnp.concatenate([before, kv, after], axis=0)
    mix, dkv = attention(starts, counts, qc, kv_ext, row_ids[None], ext_ids[None])
    from_above = lax.ppermute(dkv[:rows], "outer", down)
    from_below = lax.ppermute(dkv[2 * rows:], "outer", up)
    total = dkv[rows:2 * rows].astype(jnp.float32) + from_above.astype(jnp.float32) + from_below.astype(jnp.float32)

    def back(both):
        both = lax.all_to_all(both.reshape(rows, 1, 2 * HD), "inner", split_axis=0, concat_axis=1, tiled=True)
        return both[:, :, :HD].reshape(tok, H * HD), both[:, :, HD:].reshape(tok, H * HD)

    attended, grad_query = back(mix)
    grad_key, grad_value = back(total.astype(jnp.bfloat16))
    return attended, grad_query, grad_key, grad_value


def solution(mesh):
    rows = P(("outer", "inner"), None)
    return jax.shard_map(
        on_device, mesh=mesh,
        in_specs=(rows, rows, rows, P(("outer", "inner")), rows),
        out_specs=(rows,) * 4, check_vma=False,
    )
```

```python
import functools, math
import jax, jax.numpy as jnp
from jax import lax
from jax.sharding import PartitionSpec as P
from jax.experimental import pallas as pl
from jax.experimental.pallas import tpu as pltpu

H, HD, SAMPLES = 32, 64, 8
TQ, TK, ALIGN = 512, 512, 128
PENALTY = -float(2**20)


def attention_kernel(starts, counts, qc_ref, kv_ref, qid_ref, kid_ref, mix_ref, dkv_ref,
                     kaug, kvx, kvT, acc, pbuf, mbuf):
    rows, ext = qc_ref.shape[0], kv_ref.shape[0]
    factor = 1.0 / math.sqrt(HD)
    log2_factor = factor * math.log2(math.e)
    f32, bf16 = jnp.float32, jnp.bfloat16

    def one_hot(ids_row, width):
        sample = lax.broadcasted_iota(jnp.int32, (SAMPLES, width), 0)
        return sample == jnp.broadcast_to(ids_row, (SAMPLES, width))

    def prepare(block, _):
        at = pl.multiple_of(block * TK, TK)
        here = pl.ds(at, TK)
        tile = kv_ref[here, :]
        turned = tile.T
        kvx[here, :] = tile
        kvT[:, here] = turned
        penalty = jnp.where(one_hot(kid_ref[:, here], TK), 0.0, PENALTY)
        penalty = jnp.concatenate([penalty, jnp.zeros((HD - SAMPLES, TK), f32)], axis=0)
        kaug[here, :] = jnp.concatenate([turned[:HD], penalty.astype(bf16)], axis=0).T
        acc[here, :] = jnp.zeros((TK, 2 * HD), f32)
        return 0

    lax.fori_loop(0, ext // TK, prepare, 0)
    pad = pl.ds(ext, TK)
    lane = lax.broadcasted_iota(jnp.int32, (TK, 2 * HD), 1)
    kvx[pad, :] = jnp.zeros((TK, 2 * HD), bf16)
    kvT[:, pad] = jnp.zeros((2 * HD, TK), bf16)
    kaug[pad, :] = jnp.where((lane >= HD) & (lane < HD + SAMPLES), PENALTY, 0.0).astype(bf16)
    acc[pad, :] = jnp.zeros((TK, 2 * HD), f32)

    def query_tile(tile, _):
        q_at = pl.multiple_of(tile * TQ, TQ)
        mine = pl.ds(q_at, TQ)
        qc = qc_ref[mine, :]
        qcT = qc.T
        qT, cT = qcT[:HD], qcT[HD:]
        hot = jnp.where(one_hot(qid_ref[:, mine], TQ), 1.0, 0.0)
        hot = jnp.concatenate([hot, jnp.zeros((HD - SAMPLES, TQ), f32)], axis=0).astype(bf16)
        q_side = jnp.concatenate([qT, hot], axis=0)
        c_side = jnp.concatenate([jnp.zeros_like(cT), cT], axis=0)
        lanes = lax.broadcasted_iota(jnp.int32, qc.shape, 1)
        q_only = jnp.where(lanes < HD, qc, jnp.zeros_like(qc))
        c_only = jnp.where(lanes < HD, jnp.zeros_like(qc), qc)
        cq = jnp.concatenate([c_only, q_only], axis=0)
        first = starts[tile]
        count = counts[tile]

        def key_rows(step):
            return pl.ds(pl.multiple_of(first + step * TK, ALIGN), TK)

        def slot(step):
            return pl.ds(pl.multiple_of(step * TK, TK), TK)

        def score_step(step, state):
            top, total = state
            scores = jnp.dot(kaug[key_rows(step), :], q_side, preferred_element_type=f32) * log2_factor
            new_top = jnp.maximum(top, jnp.max(scores, axis=0, keepdims=True))
            terms = jnp.exp2(scores - new_top)
            pbuf[slot(step), :] = terms
            mbuf[step] = new_top
            return new_top, total * jnp.exp2(top - new_top) + jnp.sum(terms, axis=0, keepdims=True)

        top, total = lax.fori_loop(
            0, count, score_step, (jnp.full((1, TQ), -1e30, f32), jnp.zeros((1, TQ), f32))
        )
        scale = 1.0 / total

        def value_step(step, summed):
            weights = pbuf[slot(step), :] * (jnp.exp2(mbuf[step] - top) * scale)
            return summed + jnp.dot(
                kvT[HD:, key_rows(step)], weights.astype(bf16), preferred_element_type=f32
            )

        mixed = lax.fori_loop(0, count, value_step, jnp.zeros((HD, TQ), f32)).astype(bf16)
        row_dot = jnp.sum(cT.astype(f32) * mixed.astype(f32), axis=0, keepdims=True)

        def grad_step(step, summed):
            keys = key_rows(step)
            weights = pbuf[slot(step), :] * (jnp.exp2(mbuf[step] - top) * scale)
            grad_prob = jnp.dot(kvx[keys, :], c_side, preferred_element_type=f32)
            grad_score = (weights * (grad_prob - row_dot)).astype(bf16)
            pair = jnp.concatenate([weights.astype(bf16), grad_score], axis=1)
            acc[keys, :] += jnp.dot(pair, cq, preferred_element_type=f32)
            return summed + jnp.dot(kvT[:HD, keys], grad_score, preferred_element_type=f32)

        grad_query = lax.fori_loop(0, count, grad_step, jnp.zeros((HD, TQ), f32)) * factor
        mix_ref[mine, :] = jnp.concatenate([mixed, grad_query.astype(bf16)], axis=0).T
        return 0

    lax.fori_loop(0, rows // TQ, query_tile, 0)

    def finish(block, _):
        here = pl.ds(pl.multiple_of(block * TK, TK), TK)
        grads = acc[here, :]
        dkv_ref[here, :] = jnp.where(lane < HD, grads * factor, grads).astype(bf16)
        return 0

    lax.fori_loop(0, ext // TK, finish, 0)


def attention(starts, counts, qc, kv, qid, kid):
    rows, ext = qc.shape[0], kv.shape[0]
    vmem = pl.BlockSpec(memory_space=pltpu.VMEM)
    smem = pl.BlockSpec(memory_space=pltpu.SMEM)
    most = 2 * rows + TQ + TK + ALIGN
    return pl.pallas_call(
        attention_kernel,
        out_shape=(jax.ShapeDtypeStruct((rows, 2 * HD), jnp.bfloat16),
                   jax.ShapeDtypeStruct((ext, 2 * HD), jnp.bfloat16)),
        in_specs=[smem, smem, vmem, vmem, vmem, vmem],
        out_specs=(vmem, vmem),
        scratch_shapes=[
            pltpu.VMEM((ext + TK, 2 * HD), jnp.bfloat16),
            pltpu.VMEM((ext + TK, 2 * HD), jnp.bfloat16),
            pltpu.VMEM((2 * HD, ext + TK), jnp.bfloat16),
            pltpu.VMEM((ext + TK, 2 * HD), jnp.float32),
            pltpu.VMEM(((most + TK - 1) // TK * TK, TQ), jnp.float32),
            pltpu.VMEM(((most + TK - 1) // TK, 1, TQ), jnp.float32),
        ],
        compiler_params=pltpu.CompilerParams(vmem_limit_bytes=56 * 2**20),
        name="attention",
    )(starts, counts, qc, kv, qid, kid)


LANES = 2 * HD
MESH = pl.DeviceIdType.MESH


def partner(me, hop, size):
    return lax.rem(me + hop, size)


def packed(first, second, head):
    columns = slice(head * HD, (head + 1) * HD)
    return jnp.concatenate([first[:, columns], second[:, columns]], axis=1)


def collect_kernel(size, planes, q_ref, k_ref, v_ref, c_ref, id_ref, qc_ref, kv_ref, ids_ref,
                   qc_pack, kv_pack, own_sem, kv_send, kv_recv, qc_send, qc_recv,
                   id_send, id_recv, z_send, z_recv, zid_send, zid_recv):
    me, plane = lax.axis_index("inner"), lax.axis_index("outer")
    tok = q_ref.shape[0]
    rows = tok * size
    chunks = z_send.shape[1]
    share = size // chunks
    above, below = partner(plane, 1, planes), partner(plane, planes - 1, planes)

    barrier = pltpu.get_barrier_semaphore()

    def greet(hop, _):
        pl.semaphore_signal(barrier, inc=1, device_id={"inner": partner(me, hop, size)}, device_id_type=MESH)
        return 0

    lax.fori_loop(1, size, greet, 0)
    for other in (above, below):
        pl.semaphore_signal(barrier, inc=1, device_id={"outer": other}, device_id_type=MESH)
    for head in range(size):
        kv_pack[head] = packed(k_ref, v_ref, head)
    pl.semaphore_wait(barrier, size + 1)

    def block(owner, base=0):
        return pl.ds(pl.multiple_of(base + owner * tok, tok), tok)

    def kv_copy(other, slot):
        return pltpu.make_async_remote_copy(
            src_ref=kv_pack.at[other], dst_ref=kv_ref.at[block(slot, rows)],
            send_sem=kv_send.at[other], recv_sem=kv_recv.at[slot],
            device_id={"inner": other}, device_id_type=MESH)

    def qc_copy(other, slot):
        return pltpu.make_async_remote_copy(
            src_ref=qc_pack.at[other], dst_ref=qc_ref.at[block(slot)],
            send_sem=qc_send.at[other], recv_sem=qc_recv.at[slot],
            device_id={"inner": other}, device_id_type=MESH)

    def id_copy(other, slot):
        return pltpu.make_async_remote_copy(
            src_ref=id_ref, dst_ref=ids_ref.at[1, pl.ds(slot, 1)],
            send_sem=id_send.at[other], recv_sem=id_recv.at[slot],
            device_id={"inner": other}, device_id_type=MESH)

    own_kv = pltpu.make_async_copy(kv_pack.at[me], kv_ref.at[block(me, rows)], own_sem.at[0])
    own_id = pltpu.make_async_copy(id_ref, ids_ref.at[1, pl.ds(me, 1)], own_sem.at[1])
    own_kv.start()
    own_id.start()

    def send_kv(hop, _):
        other = partner(me, hop, size)
        kv_copy(other, me).start()
        id_copy(other, me).start()
        return 0

    lax.fori_loop(1, size, send_kv, 0)
    for head in range(size):
        qc_pack[head] = packed(q_ref, c_ref, head)
    own_qc = pltpu.make_async_copy(qc_pack.at[me], qc_ref.at[block(me)], own_sem.at[2])
    own_qc.start()

    def send_qc(hop, _):
        qc_copy(partner(me, hop, size), me).start()
        return 0

    lax.fori_loop(1, size, send_qc, 0)

    own_kv.wait()
    own_id.wait()

    def z_copies(chunk):
        src = kv_ref.at[pl.ds(pl.multiple_of(rows + chunk * (share * tok), share * tok), share * tok)]
        up = pltpu.make_async_remote_copy(
            src_ref=src, dst_ref=kv_ref.at[pl.ds(pl.multiple_of(chunk * (share * tok), share * tok), share * tok)],
            send_sem=z_send.at[0, chunk], recv_sem=z_recv.at[0, chunk],
            device_id={"outer": above}, device_id_type=MESH)
        down = pltpu.make_async_remote_copy(
            src_ref=src, dst_ref=kv_ref.at[pl.ds(pl.multiple_of(2 * rows + chunk * (share * tok), share * tok), share * tok)],
            send_sem=z_send.at[1, chunk], recv_sem=z_recv.at[1, chunk],
            device_id={"outer": below}, device_id_type=MESH)
        return up, down

    home = me // share

    def pass_on(step, _):
        chunk = lax.rem(home + chunks - step, chunks)

        def arrive(i, _):
            slot = chunk * share + i

            @pl.when(slot != me)
            def _():
                kv_copy(slot, slot).wait_recv()

            return 0

        lax.fori_loop(0, share, arrive, 0)
        for copy in z_copies(chunk):
            copy.start()
        return 0

    lax.fori_loop(0, chunks, pass_on, 0)

    def id_arrive(hop, _):
        slot = partner(me, hop, size)
        id_copy(slot, slot).wait_recv()
        return 0

    lax.fori_loop(1, size, id_arrive, 0)
    id_up = pltpu.make_async_remote_copy(
        src_ref=ids_ref.at[1], dst_ref=ids_ref.at[0], send_sem=zid_send.at[0], recv_sem=zid_recv.at[0],
        device_id={"outer": above}, device_id_type=MESH)
    id_down = pltpu.make_async_remote_copy(
        src_ref=ids_ref.at[1], dst_ref=ids_ref.at[2], send_sem=zid_send.at[1], recv_sem=zid_recv.at[1],
        device_id={"outer": below}, device_id_type=MESH)
    id_up.start()
    id_down.start()

    own_qc.wait()

    def settle(hop, _):
        slot = partner(me, hop, size)
        qc_copy(slot, slot).wait_recv()
        kv_copy(slot, me).wait_send()
        qc_copy(slot, me).wait_send()
        id_copy(slot, me).wait_send()
        return 0

    lax.fori_loop(1, size, settle, 0)
    id_up.wait()
    id_down.wait()

    def settle_z(chunk, _):
        for copy in z_copies(chunk):
            copy.wait()
        return 0

    lax.fori_loop(0, chunks, settle_z, 0)


def collect(size, planes, q, k, v, c, ids):
    tok = q.shape[0]
    rows = tok * size
    vmem = pl.BlockSpec(memory_space=pltpu.VMEM)
    hbm = pl.BlockSpec(memory_space=pl.ANY)
    dma = pltpu.SemaphoreType.DMA
    chunks = 8
    return pl.pallas_call(
        functools.partial(collect_kernel, size, planes),
        out_shape=(jax.ShapeDtypeStruct((rows, LANES), jnp.bfloat16),
                   jax.ShapeDtypeStruct((3 * rows, LANES), jnp.bfloat16),
                   jax.ShapeDtypeStruct((3, size, tok), jnp.int32)),
        in_specs=[vmem] * 5,
        out_specs=(hbm, hbm, vmem),
        scratch_shapes=[
            pltpu.VMEM((size, tok, LANES), jnp.bfloat16),
            pltpu.VMEM((size, tok, LANES), jnp.bfloat16),
            dma((3,)), dma((size,)), dma((size,)), dma((size,)), dma((size,)),
            dma((size,)), dma((size,)), dma((2, chunks)), dma((2, chunks)), dma((2,)), dma((2,)),
        ],
        compiler_params=pltpu.CompilerParams(collective_id=0, has_side_effects=True, vmem_limit_bytes=32 * 2**20),
        name="collect",
    )(q, k, v, c, ids)


def return_kernel(size, planes, mix_ref, dkv_ref, rmix_ref, rkv_ref, from_z, total,
                  own_sem, mix_send, mix_recv, kv_send, kv_recv, z_send, z_recv):
    me, plane = lax.axis_index("inner"), lax.axis_index("outer")
    rows = mix_ref.shape[0]
    tok = rows // size
    chunks = z_send.shape[1]
    share = size // chunks
    step_rows = share * tok
    above, below = partner(plane, 1, planes), partner(plane, planes - 1, planes)
    barrier = pltpu.get_barrier_semaphore()

    def greet(hop, _):
        pl.semaphore_signal(barrier, inc=1, device_id={"inner": partner(me, hop, size)}, device_id_type=MESH)
        return 0

    lax.fori_loop(1, size, greet, 0)
    for other in (above, below):
        pl.semaphore_signal(barrier, inc=1, device_id={"outer": other}, device_id_type=MESH)
    pl.semaphore_wait(barrier, size + 1)

    def block(owner):
        return pl.ds(pl.multiple_of(owner * tok, tok), tok)

    def part(chunk, base=0):
        return pl.ds(pl.multiple_of(base + chunk * step_rows, step_rows), step_rows)

    def z_copies(chunk):
        down = pltpu.make_async_remote_copy(
            src_ref=dkv_ref.at[part(chunk)], dst_ref=from_z.at[0, part(chunk)],
            send_sem=z_send.at[0, chunk], recv_sem=z_recv.at[0, chunk],
            device_id={"outer": below}, device_id_type=MESH)
        up = pltpu.make_async_remote_copy(
            src_ref=dkv_ref.at[part(chunk, 2 * rows)], dst_ref=from_z.at[1, part(chunk)],
            send_sem=z_send.at[1, chunk], recv_sem=z_recv.at[1, chunk],
            device_id={"outer": above}, device_id_type=MESH)
        return down, up

    def mix_copy(other, slot):
        return pltpu.make_async_remote_copy(
            src_ref=mix_ref.at[block(other)], dst_ref=rmix_ref.at[slot],
            send_sem=mix_send.at[other], recv_sem=mix_recv.at[slot],
            device_id={"inner": other}, device_id_type=MESH)

    def kv_copy(other, slot):
        return pltpu.make_async_remote_copy(
            src_ref=total.at[block(other)], dst_ref=rkv_ref.at[slot],
            send_sem=kv_send.at[other], recv_sem=kv_recv.at[slot],
            device_id={"inner": other}, device_id_type=MESH)

    home = me // share

    def send_z(step, _):
        for copy in z_copies(lax.rem(home + step, chunks)):
            copy.start()
        return 0

    lax.fori_loop(0, chunks, send_z, 0)
    own_mix = pltpu.make_async_copy(mix_ref.at[block(me)], rmix_ref.at[me], own_sem.at[0])
    own_mix.start()

    def send_mix(hop, _):
        mix_copy(partner(me, hop, size), me).start()
        return 0

    lax.fori_loop(1, size, send_mix, 0)
    own_kv = pltpu.make_async_copy(total.at[block(me)], rkv_ref.at[me], own_sem.at[1])

    def add_up(step, _):
        chunk = lax.rem(home + step, chunks)
        for copy in z_copies(chunk):
            copy.wait_recv()
        mine = dkv_ref[part(chunk, rows), :].astype(jnp.float32)
        first = from_z[0, part(chunk), :].astype(jnp.float32)
        second = from_z[1, part(chunk), :].astype(jnp.float32)
        total[part(chunk), :] = (mine + first + second).astype(jnp.bfloat16)

        def send(i, _):
            other = chunk * share + i

            @pl.when(other != me)
            def _():
                kv_copy(other, me).start()

            @pl.when(other == me)
            def _():
                own_kv.start()

            return 0

        lax.fori_loop(0, share, send, 0)
        return 0

    lax.fori_loop(0, chunks, add_up, 0)
    own_mix.wait()
    own_kv.wait()

    def settle(hop, _):
        slot = partner(me, hop, size)
        mix_copy(slot, slot).wait_recv()
        kv_copy(slot, slot).wait_recv()
        mix_copy(slot, me).wait_send()
        kv_copy(slot, me).wait_send()
        return 0

    lax.fori_loop(1, size, settle, 0)

    def settle_z(chunk, _):
        for copy in z_copies(chunk):
            copy.wait_send()
        return 0

    lax.fori_loop(0, chunks, settle_z, 0)


def give_back(size, planes, mix, dkv):
    rows = mix.shape[0]
    tok = rows // size
    vmem = pl.BlockSpec(memory_space=pltpu.VMEM)
    hbm = pl.BlockSpec(memory_space=pl.ANY)
    dma = pltpu.SemaphoreType.DMA
    chunks = 8
    got = jax.ShapeDtypeStruct((size, tok, LANES), jnp.bfloat16)
    return pl.pallas_call(
        functools.partial(return_kernel, size, planes),
        out_shape=(got, got),
        in_specs=[vmem, vmem],
        out_specs=(hbm, hbm),
        scratch_shapes=[
            pltpu.VMEM((2, rows, LANES), jnp.bfloat16),
            pltpu.VMEM((rows, LANES), jnp.bfloat16),
            dma((2,)), dma((size,)), dma((size,)), dma((size,)), dma((size,)), dma((2, chunks)), dma((2, chunks)),
        ],
        compiler_params=pltpu.CompilerParams(collective_id=1, has_side_effects=True, vmem_limit_bytes=32 * 2**20),
        name="give_back",
    )(mix, dkv)


def unpack_kernel(rmix_ref, rkv_ref, att_ref, dq_ref, dk_ref, dv_ref):
    for head in range(rmix_ref.shape[0]):
        columns = slice(head * HD, (head + 1) * HD)
        mix, grads = rmix_ref[head], rkv_ref[head]
        att_ref[:, columns] = mix[:, :HD]
        dq_ref[:, columns] = mix[:, HD:]
        dk_ref[:, columns] = grads[:, :HD]
        dv_ref[:, columns] = grads[:, HD:]


def unpack(rmix, rkv):
    heads, tok, _ = rmix.shape
    vmem = pl.BlockSpec(memory_space=pltpu.VMEM)
    return pl.pallas_call(
        unpack_kernel,
        out_shape=(jax.ShapeDtypeStruct((tok, heads * HD), jnp.bfloat16),) * 4,
        in_specs=[vmem, vmem],
        out_specs=(vmem,) * 4,
        compiler_params=pltpu.CompilerParams(vmem_limit_bytes=32 * 2**20),
        name="unpack",
    )(rmix, rkv)


def on_device(query_rows, key_rows, value_rows, sample_of, cotangent):
    size, planes = lax.axis_size("inner"), lax.axis_size("outer")
    tok = query_rows.shape[0]
    rows = tok * size
    qc, kv, ids = collect(size, planes, query_rows, key_rows, value_rows, cotangent, sample_of[None])
    group = lax.axis_index("outer")
    before = jnp.where(group == 0, -1, ids[0])
    after = jnp.where(group == planes - 1, SAMPLES, ids[2])
    row_ids = ids[1].reshape(rows)
    ext_ids = jnp.concatenate([before.reshape(rows), row_ids, after.reshape(rows)])
    tiles = row_ids.reshape(rows // TQ, TQ)
    low = jnp.sum((ext_ids[None, :] < tiles[:, :1]).astype(jnp.int32), axis=1)
    high = jnp.sum((ext_ids[None, :] <= tiles[:, -1:]).astype(jnp.int32), axis=1)
    starts = low // ALIGN * ALIGN
    counts = (high - starts + TK - 1) // TK
    mix, dkv = attention(starts, counts, qc, kv, row_ids[None], ext_ids[None])
    return unpack(*give_back(size, planes, mix, dkv))


def solution(mesh):
    rows = P(("outer", "inner"), None)
    return jax.shard_map(
        on_device, mesh=mesh,
        in_specs=(rows, rows, rows, P(("outer", "inner")), rows),
        out_specs=(rows,) * 4, check_vma=False,
    )
```

```python
import functools, math
import jax, jax.numpy as jnp
from jax import lax
from jax.sharding import PartitionSpec as P
from jax.experimental import pallas as pl
from jax.experimental.pallas import tpu as pltpu

HD, SAMPLES = 64, 8
LANES = 2 * HD
MESH = pl.DeviceIdType.MESH
TQ, TK, BLOCK, ALIGN = 512, 256, 512, 128
LEVELS = (8, 2, 1)
PENALTY = -float(2**20)
SAFE_POWER = 100.0


def looped(count, step, state):
    done = 0
    for level in LEVELS:

        def several(turn, state, level=level, done=done):
            for i in range(level):
                state = step(done + turn * level + i, state)
            return state

        turns = (count - done) // level
        state = lax.fori_loop(0, turns, several, state)
        done = done + turns * level
    return state


def attention_kernel(planes, qc_ref, kv_ref, ids_ref, mix_ref, dkv_ref,
                     kid, kaug, kvx, kvT, acc, pbuf, mbuf, edges):
    f32, bf16, i32 = jnp.float32, jnp.bfloat16, jnp.int32
    rows, ext = qc_ref.shape[0], kv_ref.shape[0]
    _, owners, tok = ids_ref.shape
    per_block = BLOCK // tok
    factor = 1.0 / math.sqrt(HD)
    log2_factor = factor * math.log2(math.e)
    plane = lax.axis_index("outer")

    before = jnp.where(plane == 0, -1, ids_ref[0])
    after = jnp.where(plane == planes - 1, SAMPLES, ids_ref[2])
    parts = (before, ids_ref[1], after)
    for sample in range(SAMPLES + 1):
        low = sum((part < sample).astype(i32) for part in parts)
        edges[sample] = jnp.sum(low)
    for place, part in enumerate(parts):
        for owner in range(owners):
            at = place * owners + owner
            kid[at // per_block, :, (at % per_block) * tok:(at % per_block + 1) * tok] = part[owner:owner + 1]

    def span(begin, end):
        first, last = edges[0] * 0, edges[0] * 0 + ext
        for sample in range(SAMPLES + 1):
            edge = edges[sample]
            first = jnp.where(edge <= begin, jnp.maximum(first, edge), first)
            last = jnp.where(edge >= end, jnp.minimum(last, edge), last)
        return first, last

    def one_hot(ids_row):
        width = ids_row.shape[1]
        sample = lax.broadcasted_iota(i32, (SAMPLES, width), 0)
        return sample == jnp.broadcast_to(ids_row, (SAMPLES, width))

    lane = lax.broadcasted_iota(i32, (BLOCK, LANES), 1)

    def clear(block, _):
        acc[pl.ds(pl.multiple_of(block * BLOCK, BLOCK), BLOCK), :] = jnp.zeros((BLOCK, LANES), f32)
        return 0

    lax.fori_loop(0, acc.shape[0] // BLOCK, clear, 0)

    def squared(turned):
        wide = turned.astype(f32)
        return jnp.sum(wide * wide, axis=0, keepdims=True)

    def prepare(block, largest):
        here = pl.ds(pl.multiple_of(block * BLOCK, BLOCK), BLOCK)
        tile = kv_ref[here, :]
        turned = tile.T
        kvx[here, :] = tile
        kvT[:, here] = turned
        penalty = jnp.where(one_hot(kid[block]), 0.0, PENALTY)
        penalty = jnp.concatenate([penalty, jnp.zeros((HD - SAMPLES, BLOCK), f32)], axis=0)
        kaug[here, :] = jnp.concatenate([turned[:HD], penalty.astype(bf16)], axis=0).T
        return jnp.maximum(largest, squared(turned[:HD]))

    reach_first, reach_last = span(rows, 2 * rows)
    first_block = reach_first // BLOCK
    last_block = (reach_last + BLOCK - 1) // BLOCK
    key_square = lax.fori_loop(first_block, last_block, prepare, jnp.zeros((1, BLOCK), f32))
    key_most = jnp.max(key_square)

    def pad(block):
        here = pl.ds(pl.multiple_of(block * BLOCK, BLOCK), BLOCK)
        kvx[here, :] = jnp.zeros((BLOCK, LANES), bf16)
        kvT[:, here] = jnp.zeros((LANES, BLOCK), bf16)
        kaug[here, :] = jnp.where((lane >= HD) & (lane < HD + SAMPLES), PENALTY, 0.0).astype(bf16)

    pad(last_block)

    def query_tile(tile, _):
        q_at = pl.multiple_of(tile * TQ, TQ)
        mine = pl.ds(q_at, TQ)
        qc = qc_ref[mine, :]
        qcT = qc.T
        qT, cT = qcT[:HD], qcT[HD:]
        own = [kid[(rows + q_at) // BLOCK + i] for i in range(TQ // BLOCK)]
        own = own[0] if len(own) == 1 else jnp.concatenate(own, axis=1)
        hot = jnp.where(one_hot(own), 1.0, 0.0)
        hot = jnp.concatenate([hot, jnp.zeros((HD - SAMPLES, TQ), f32)], axis=0).astype(bf16)
        q_side = jnp.concatenate([qT, hot], axis=0)
        c_side = jnp.concatenate([jnp.zeros_like(cT), cT], axis=0)
        lanes = lax.broadcasted_iota(i32, qc.shape, 1)
        q_only = jnp.where(lanes < HD, qc, jnp.zeros_like(qc))
        c_only = jnp.where(lanes < HD, jnp.zeros_like(qc), qc)
        cq = jnp.concatenate([c_only, q_only], axis=0)
        begin, end = span(rows + q_at, rows + q_at + TQ)
        first = begin // ALIGN * ALIGN
        count = (end - first + TK - 1) // TK

        def key_rows(step):
            return pl.ds(pl.multiple_of(first + step * TK, ALIGN), TK)

        def slot(step):
            return pl.ds(pl.multiple_of(step * TK, TK), TK)

        def scores_of(step):
            return jnp.dot(kaug[key_rows(step), :], q_side, preferred_element_type=f32) * log2_factor

        def bounded_step(step, total):
            terms = jnp.exp2(scores_of(step))
            pbuf[slot(step), :] = terms
            mbuf[step] = jnp.zeros((1, TQ), f32)
            return total + jnp.sum(terms, axis=0, keepdims=True)

        def running_step(step, state):
            top, total = state
            scores = scores_of(step)
            new_top = jnp.maximum(top, jnp.max(scores, axis=0, keepdims=True))
            terms = jnp.exp2(scores - new_top)
            pbuf[slot(step), :] = terms
            mbuf[step] = new_top
            return new_top, total * jnp.exp2(top - new_top) + jnp.sum(terms, axis=0, keepdims=True)

        def bounded():
            return jnp.zeros((1, TQ), f32), looped(count, bounded_step, jnp.zeros((1, TQ), f32))

        def running():
            start = (jnp.full((1, TQ), -1e30, f32), jnp.zeros((1, TQ), f32))
            return lax.fori_loop(0, count, running_step, start)

        query_most = jnp.max(squared(qT))
        small = query_most * key_most <= (SAFE_POWER / log2_factor) ** 2
        top, total = lax.cond(small, bounded, running)
        scale = 1.0 / total

        def weights_of(step):
            return pbuf[slot(step), :] * (jnp.exp2(mbuf[step] - top) * scale)

        def value_step(step, summed):
            return summed + jnp.dot(
                kvT[HD:, key_rows(step)], weights_of(step).astype(bf16), preferred_element_type=f32
            )

        mixed = looped(count, value_step, jnp.zeros((HD, TQ), f32)).astype(bf16)
        row_dot = jnp.sum(cT.astype(f32) * mixed.astype(f32), axis=0, keepdims=True)

        def grad_step(step, summed):
            keys = key_rows(step)
            weights = weights_of(step)
            grad_prob = jnp.dot(kvx[keys, :], c_side, preferred_element_type=f32)
            grad_score = (weights * (grad_prob - row_dot)).astype(bf16)
            pair = jnp.concatenate([weights.astype(bf16), grad_score], axis=1)
            acc[keys, :] += jnp.dot(pair, cq, preferred_element_type=f32)
            return summed + jnp.dot(kvT[:HD, keys], grad_score, preferred_element_type=f32)

        grad_query = looped(count, grad_step, jnp.zeros((HD, TQ), f32)) * factor
        mix_ref[mine, :] = jnp.concatenate([mixed, grad_query.astype(bf16)], axis=0).T
        return 0

    lax.fori_loop(0, rows // TQ, query_tile, 0)

    def finish(block, _):
        here = pl.ds(pl.multiple_of(block * BLOCK, BLOCK), BLOCK)
        grads = acc[here, :]
        dkv_ref[here, :] = jnp.where(lane < HD, grads * factor, grads).astype(bf16)
        return 0

    lax.fori_loop(0, ext // BLOCK, finish, 0)


def attention(planes, qc, kv, ids):
    rows, ext = qc.shape[0], kv.shape[0]
    vmem = pl.BlockSpec(memory_space=pltpu.VMEM)
    padded = ext + max(TK, BLOCK)
    steps = (2 * rows + TQ + TK + ALIGN) // TK
    bf16, f32 = jnp.bfloat16, jnp.float32
    return pl.pallas_call(
        functools.partial(attention_kernel, planes),
        out_shape=(jax.ShapeDtypeStruct((rows, LANES), bf16),
                   jax.ShapeDtypeStruct((ext, LANES), bf16)),
        in_specs=[vmem] * 3,
        out_specs=(vmem, vmem),
        scratch_shapes=[
            pltpu.VMEM((ext // BLOCK, 1, BLOCK), jnp.int32),
            pltpu.VMEM((padded, LANES), bf16),
            pltpu.VMEM((padded, LANES), bf16),
            pltpu.VMEM((LANES, padded), bf16),
            pltpu.VMEM((padded, LANES), f32),
            pltpu.VMEM((steps * TK, TQ), f32),
            pltpu.VMEM((steps, 1, TQ), f32),
            pltpu.SMEM((SAMPLES + 1,), jnp.int32),
        ],
        compiler_params=pltpu.CompilerParams(vmem_limit_bytes=60 * 2**20),
        name="attention",
    )(qc, kv, ids)


def partner(me, hop, size):
    return lax.rem(me + hop, size)


def packed(first, second, head):
    columns = slice(head * HD, (head + 1) * HD)
    return jnp.concatenate([first[:, columns], second[:, columns]], axis=1)


def collect_kernel(size, planes, q_ref, k_ref, v_ref, c_ref, id_ref, qc_ref, kv_ref, ids_ref,
                   qc_pack, kv_pack, own_sem, kv_send, kv_recv, qc_send, qc_recv,
                   id_send, id_recv, z_send, z_recv, zid_send, zid_recv):
    me, plane = lax.axis_index("inner"), lax.axis_index("outer")
    tok = q_ref.shape[0]
    rows = tok * size
    chunks = z_send.shape[1]
    share = size // chunks
    above, below = partner(plane, 1, planes), partner(plane, planes - 1, planes)

    barrier = pltpu.get_barrier_semaphore()

    def greet(hop, _):
        pl.semaphore_signal(barrier, inc=1, device_id={"inner": partner(me, hop, size)}, device_id_type=MESH)
        return 0

    lax.fori_loop(1, size, greet, 0)
    for other in (above, below):
        pl.semaphore_signal(barrier, inc=1, device_id={"outer": other}, device_id_type=MESH)
    for head in range(size):
        kv_pack[head] = packed(k_ref, v_ref, head)
    pl.semaphore_wait(barrier, size + 1)

    def block(owner, base=0):
        return pl.ds(pl.multiple_of(base + owner * tok, tok), tok)

    def kv_copy(other, slot):
        return pltpu.make_async_remote_copy(
            src_ref=kv_pack.at[other], dst_ref=kv_ref.at[block(slot, rows)],
            send_sem=kv_send.at[other], recv_sem=kv_recv.at[slot],
            device_id={"inner": other}, device_id_type=MESH)

    def qc_copy(other, slot):
        return pltpu.make_async_remote_copy(
            src_ref=qc_pack.at[other], dst_ref=qc_ref.at[block(slot)],
            send_sem=qc_send.at[other], recv_sem=qc_recv.at[slot],
            device_id={"inner": other}, device_id_type=MESH)

    def id_copy(other, slot):
        return pltpu.make_async_remote_copy(
            src_ref=id_ref, dst_ref=ids_ref.at[1, pl.ds(slot, 1)],
            send_sem=id_send.at[other], recv_sem=id_recv.at[slot],
            device_id={"inner": other}, device_id_type=MESH)

    own_kv = pltpu.make_async_copy(kv_pack.at[me], kv_ref.at[block(me, rows)], own_sem.at[0])
    own_id = pltpu.make_async_copy(id_ref, ids_ref.at[1, pl.ds(me, 1)], own_sem.at[1])
    own_kv.start()
    own_id.start()

    def send_kv(hop, _):
        other = partner(me, hop, size)
        kv_copy(other, me).start()
        id_copy(other, me).start()
        return 0

    lax.fori_loop(1, size, send_kv, 0)
    for head in range(size):
        qc_pack[head] = packed(q_ref, c_ref, head)
    own_qc = pltpu.make_async_copy(qc_pack.at[me], qc_ref.at[block(me)], own_sem.at[2])
    own_qc.start()

    def send_qc(hop, _):
        qc_copy(partner(me, hop, size), me).start()
        return 0

    lax.fori_loop(1, size, send_qc, 0)

    own_kv.wait()
    own_id.wait()

    def z_copies(chunk):
        src = kv_ref.at[pl.ds(pl.multiple_of(rows + chunk * (share * tok), share * tok), share * tok)]
        up = pltpu.make_async_remote_copy(
            src_ref=src, dst_ref=kv_ref.at[pl.ds(pl.multiple_of(chunk * (share * tok), share * tok), share * tok)],
            send_sem=z_send.at[0, chunk], recv_sem=z_recv.at[0, chunk],
            device_id={"outer": above}, device_id_type=MESH)
        down = pltpu.make_async_remote_copy(
            src_ref=src, dst_ref=kv_ref.at[pl.ds(pl.multiple_of(2 * rows + chunk * (share * tok), share * tok), share * tok)],
            send_sem=z_send.at[1, chunk], recv_sem=z_recv.at[1, chunk],
            device_id={"outer": below}, device_id_type=MESH)
        return up, down

    home = me // share

    def pass_on(step, _):
        chunk = lax.rem(home + chunks - step, chunks)

        def arrive(i, _):
            slot = chunk * share + i

            @pl.when(slot != me)
            def _():
                kv_copy(slot, slot).wait_recv()

            return 0

        lax.fori_loop(0, share, arrive, 0)
        for copy in z_copies(chunk):
            copy.start()
        return 0

    lax.fori_loop(0, chunks, pass_on, 0)

    def id_arrive(hop, _):
        slot = partner(me, hop, size)
        id_copy(slot, slot).wait_recv()
        return 0

    lax.fori_loop(1, size, id_arrive, 0)
    id_up = pltpu.make_async_remote_copy(
        src_ref=ids_ref.at[1], dst_ref=ids_ref.at[0], send_sem=zid_send.at[0], recv_sem=zid_recv.at[0],
        device_id={"outer": above}, device_id_type=MESH)
    id_down = pltpu.make_async_remote_copy(
        src_ref=ids_ref.at[1], dst_ref=ids_ref.at[2], send_sem=zid_send.at[1], recv_sem=zid_recv.at[1],
        device_id={"outer": below}, device_id_type=MESH)
    id_up.start()
    id_down.start()

    own_qc.wait()

    def settle(hop, _):
        slot = partner(me, hop, size)
        qc_copy(slot, slot).wait_recv()
        kv_copy(slot, me).wait_send()
        qc_copy(slot, me).wait_send()
        id_copy(slot, me).wait_send()
        return 0

    lax.fori_loop(1, size, settle, 0)
    id_up.wait()
    id_down.wait()

    def settle_z(chunk, _):
        for copy in z_copies(chunk):
            copy.wait()
        return 0

    lax.fori_loop(0, chunks, settle_z, 0)


def collect(size, planes, q, k, v, c, ids):
    tok = q.shape[0]
    rows = tok * size
    vmem = pl.BlockSpec(memory_space=pltpu.VMEM)
    hbm = pl.BlockSpec(memory_space=pl.ANY)
    dma = pltpu.SemaphoreType.DMA
    chunks = 8
    return pl.pallas_call(
        functools.partial(collect_kernel, size, planes),
        out_shape=(jax.ShapeDtypeStruct((rows, LANES), jnp.bfloat16),
                   jax.ShapeDtypeStruct((3 * rows, LANES), jnp.bfloat16),
                   jax.ShapeDtypeStruct((3, size, tok), jnp.int32)),
        in_specs=[vmem] * 5,
        out_specs=(hbm, hbm, vmem),
        scratch_shapes=[
            pltpu.VMEM((size, tok, LANES), jnp.bfloat16),
            pltpu.VMEM((size, tok, LANES), jnp.bfloat16),
            dma((3,)), dma((size,)), dma((size,)), dma((size,)), dma((size,)),
            dma((size,)), dma((size,)), dma((2, chunks)), dma((2, chunks)), dma((2,)), dma((2,)),
        ],
        compiler_params=pltpu.CompilerParams(collective_id=0, has_side_effects=True, vmem_limit_bytes=32 * 2**20),
        name="collect",
    )(q, k, v, c, ids)


def return_kernel(size, planes, mix_ref, dkv_ref, rmix_ref, rkv_ref, from_z, total,
                  own_sem, mix_send, mix_recv, kv_send, kv_recv, z_send, z_recv):
    me, plane = lax.axis_index("inner"), lax.axis_index("outer")
    rows = mix_ref.shape[0]
    tok = rows // size
    chunks = z_send.shape[1]
    share = size // chunks
    step_rows = share * tok
    above, below = partner(plane, 1, planes), partner(plane, planes - 1, planes)
    barrier = pltpu.get_barrier_semaphore()

    def greet(hop, _):
        pl.semaphore_signal(barrier, inc=1, device_id={"inner": partner(me, hop, size)}, device_id_type=MESH)
        return 0

    lax.fori_loop(1, size, greet, 0)
    for other in (above, below):
        pl.semaphore_signal(barrier, inc=1, device_id={"outer": other}, device_id_type=MESH)
    pl.semaphore_wait(barrier, size + 1)

    def block(owner):
        return pl.ds(pl.multiple_of(owner * tok, tok), tok)

    def part(chunk, base=0):
        return pl.ds(pl.multiple_of(base + chunk * step_rows, step_rows), step_rows)

    def z_copies(chunk):
        down = pltpu.make_async_remote_copy(
            src_ref=dkv_ref.at[part(chunk)], dst_ref=from_z.at[0, part(chunk)],
            send_sem=z_send.at[0, chunk], recv_sem=z_recv.at[0, chunk],
            device_id={"outer": below}, device_id_type=MESH)
        up = pltpu.make_async_remote_copy(
            src_ref=dkv_ref.at[part(chunk, 2 * rows)], dst_ref=from_z.at[1, part(chunk)],
            send_sem=z_send.at[1, chunk], recv_sem=z_recv.at[1, chunk],
            device_id={"outer": above}, device_id_type=MESH)
        return down, up

    def mix_copy(other, slot):
        return pltpu.make_async_remote_copy(
            src_ref=mix_ref.at[block(other)], dst_ref=rmix_ref.at[slot],
            send_sem=mix_send.at[other], recv_sem=mix_recv.at[slot],
            device_id={"inner": other}, device_id_type=MESH)

    def kv_copy(other, slot):
        return pltpu.make_async_remote_copy(
            src_ref=total.at[block(other)], dst_ref=rkv_ref.at[slot],
            send_sem=kv_send.at[other], recv_sem=kv_recv.at[slot],
            device_id={"inner": other}, device_id_type=MESH)

    home = me // share

    def send_z(step, _):
        for copy in z_copies(lax.rem(home + step, chunks)):
            copy.start()
        return 0

    lax.fori_loop(0, chunks, send_z, 0)
    own_mix = pltpu.make_async_copy(mix_ref.at[block(me)], rmix_ref.at[me], own_sem.at[0])
    own_mix.start()

    def send_mix(hop, _):
        mix_copy(partner(me, hop, size), me).start()
        return 0

    lax.fori_loop(1, size, send_mix, 0)
    own_kv = pltpu.make_async_copy(total.at[block(me)], rkv_ref.at[me], own_sem.at[1])

    def add_up(step, _):
        chunk = lax.rem(home + step, chunks)
        for copy in z_copies(chunk):
            copy.wait_recv()
        mine = dkv_ref[part(chunk, rows), :].astype(jnp.float32)
        first = from_z[0, part(chunk), :].astype(jnp.float32)
        second = from_z[1, part(chunk), :].astype(jnp.float32)
        total[part(chunk), :] = (mine + first + second).astype(jnp.bfloat16)

        def send(i, _):
            other = chunk * share + i

            @pl.when(other != me)
            def _():
                kv_copy(other, me).start()

            @pl.when(other == me)
            def _():
                own_kv.start()

            return 0

        lax.fori_loop(0, share, send, 0)
        return 0

    lax.fori_loop(0, chunks, add_up, 0)
    own_mix.wait()
    own_kv.wait()

    def settle(hop, _):
        slot = partner(me, hop, size)
        mix_copy(slot, slot).wait_recv()
        kv_copy(slot, slot).wait_recv()
        mix_copy(slot, me).wait_send()
        kv_copy(slot, me).wait_send()
        return 0

    lax.fori_loop(1, size, settle, 0)

    def settle_z(chunk, _):
        for copy in z_copies(chunk):
            copy.wait_send()
        return 0

    lax.fori_loop(0, chunks, settle_z, 0)


def give_back(size, planes, mix, dkv):
    rows = mix.shape[0]
    tok = rows // size
    vmem = pl.BlockSpec(memory_space=pltpu.VMEM)
    hbm = pl.BlockSpec(memory_space=pl.ANY)
    dma = pltpu.SemaphoreType.DMA
    chunks = 8
    got = jax.ShapeDtypeStruct((size, tok, LANES), jnp.bfloat16)
    return pl.pallas_call(
        functools.partial(return_kernel, size, planes),
        out_shape=(got, got),
        in_specs=[vmem, vmem],
        out_specs=(hbm, hbm),
        scratch_shapes=[
            pltpu.VMEM((2, rows, LANES), jnp.bfloat16),
            pltpu.VMEM((rows, LANES), jnp.bfloat16),
            dma((2,)), dma((size,)), dma((size,)), dma((size,)), dma((size,)), dma((2, chunks)), dma((2, chunks)),
        ],
        compiler_params=pltpu.CompilerParams(collective_id=1, has_side_effects=True, vmem_limit_bytes=32 * 2**20),
        name="give_back",
    )(mix, dkv)


def unpack_kernel(rmix_ref, rkv_ref, att_ref, dq_ref, dk_ref, dv_ref):
    for head in range(rmix_ref.shape[0]):
        columns = slice(head * HD, (head + 1) * HD)
        mix, grads = rmix_ref[head], rkv_ref[head]
        att_ref[:, columns] = mix[:, :HD]
        dq_ref[:, columns] = mix[:, HD:]
        dk_ref[:, columns] = grads[:, :HD]
        dv_ref[:, columns] = grads[:, HD:]


def unpack(rmix, rkv):
    heads, tok, _ = rmix.shape
    vmem = pl.BlockSpec(memory_space=pltpu.VMEM)
    return pl.pallas_call(
        unpack_kernel,
        out_shape=(jax.ShapeDtypeStruct((tok, heads * HD), jnp.bfloat16),) * 4,
        in_specs=[vmem, vmem],
        out_specs=(vmem,) * 4,
        compiler_params=pltpu.CompilerParams(vmem_limit_bytes=32 * 2**20),
        name="unpack",
    )(rmix, rkv)


def on_device(query_rows, key_rows, value_rows, sample_of, cotangent):
    size, planes = lax.axis_size("inner"), lax.axis_size("outer")
    qc, kv, ids = collect(size, planes, query_rows, key_rows, value_rows, cotangent, sample_of[None])
    mix, dkv = attention(planes, qc, kv, ids)
    return unpack(*give_back(size, planes, mix, dkv))


def solution(mesh):
    rows = P(("outer", "inner"), None)
    return jax.shard_map(
        on_device, mesh=mesh,
        in_specs=(rows, rows, rows, P(("outer", "inner")), rows),
        out_specs=(rows,) * 4, check_vma=False,
    )
```

```python
import functools, math
import jax, jax.numpy as jnp
from jax import lax
from jax.sharding import PartitionSpec as P
from jax.experimental import pallas as pl
from jax.experimental.pallas import tpu as pltpu

HD, SAMPLES = 64, 8
LANES = 2 * HD
MESH = pl.DeviceIdType.MESH
TQ, TK, BLOCK, ALIGN = 512, 256, 512, 128
LEVELS = (8, 2, 1)
PENALTY = -float(2**20)
SAFE_POWER = 100.0


def looped(count, step, state):
    done = 0
    for level in LEVELS:

        def several(turn, state, level=level, done=done):
            for i in range(level):
                state = step(done + turn * level + i, state)
            return state

        turns = (count - done) // level
        state = lax.fori_loop(0, turns, several, state)
        done = done + turns * level
    return state


def attention_kernel(planes, qc_hbm, kv_hbm, ids_ref, mix_hbm, dkv_hbm,
                     qc_ref, mix_ref, dkv_ref, kid, kaug, kvx, kvT, acc, pbuf, mbuf, edges,
                     in_sem, mix_sem, dkv_sem):
    f32, bf16, i32 = jnp.float32, jnp.bfloat16, jnp.int32
    rows, ext = qc_hbm.shape[0], kv_hbm.shape[0]
    kv_in = pltpu.make_async_copy(kv_hbm, kvx.at[pl.ds(0, ext)], in_sem.at[0])
    qc_in = pltpu.make_async_copy(qc_hbm, qc_ref, in_sem.at[1])
    kv_in.start()
    qc_in.start()
    _, owners, tok = ids_ref.shape
    per_block = BLOCK // tok
    factor = 1.0 / math.sqrt(HD)
    log2_factor = factor * math.log2(math.e)
    plane = lax.axis_index("outer")

    before = jnp.where(plane == 0, -1, ids_ref[0])
    after = jnp.where(plane == planes - 1, SAMPLES, ids_ref[2])
    parts = (before, ids_ref[1], after)
    for sample in range(SAMPLES + 1):
        low = sum((part < sample).astype(i32) for part in parts)
        edges[sample] = jnp.sum(low)
    for place, part in enumerate(parts):
        for owner in range(owners):
            at = place * owners + owner
            kid[at // per_block, :, (at % per_block) * tok:(at % per_block + 1) * tok] = part[owner:owner + 1]

    def span(begin, end):
        first, last = edges[0] * 0, edges[0] * 0 + ext
        for sample in range(SAMPLES + 1):
            edge = edges[sample]
            first = jnp.where(edge <= begin, jnp.maximum(first, edge), first)
            last = jnp.where(edge >= end, jnp.minimum(last, edge), last)
        return first, last

    def one_hot(ids_row):
        width = ids_row.shape[1]
        sample = lax.broadcasted_iota(i32, (SAMPLES, width), 0)
        return sample == jnp.broadcast_to(ids_row, (SAMPLES, width))

    lane = lax.broadcasted_iota(i32, (BLOCK, LANES), 1)

    def clear(block, _):
        acc[pl.ds(pl.multiple_of(block * BLOCK, BLOCK), BLOCK), :] = jnp.zeros((BLOCK, LANES), f32)
        return 0

    lax.fori_loop(0, acc.shape[0] // BLOCK, clear, 0)

    def squared(turned):
        wide = turned.astype(f32)
        return jnp.sum(wide * wide, axis=0, keepdims=True)

    def prepare(block, largest):
        here = pl.ds(pl.multiple_of(block * BLOCK, BLOCK), BLOCK)
        turned = kvx[here, :].T
        kvT[:, here] = turned
        penalty = jnp.where(one_hot(kid[block]), 0.0, PENALTY)
        penalty = jnp.concatenate([penalty, jnp.zeros((HD - SAMPLES, BLOCK), f32)], axis=0)
        kaug[here, :] = jnp.concatenate([turned[:HD], penalty.astype(bf16)], axis=0).T
        return jnp.maximum(largest, squared(turned[:HD]))

    kv_in.wait()
    reach_first, reach_last = span(rows, 2 * rows)
    first_block = reach_first // BLOCK
    last_block = (reach_last + BLOCK - 1) // BLOCK
    key_square = lax.fori_loop(first_block, last_block, prepare, jnp.zeros((1, BLOCK), f32))
    key_most = jnp.max(key_square)

    def pad(block):
        here = pl.ds(pl.multiple_of(block * BLOCK, BLOCK), BLOCK)
        kvx[here, :] = jnp.zeros((BLOCK, LANES), bf16)
        kvT[:, here] = jnp.zeros((LANES, BLOCK), bf16)
        kaug[here, :] = jnp.where((lane >= HD) & (lane < HD + SAMPLES), PENALTY, 0.0).astype(bf16)

    pad(last_block)
    qc_in.wait()

    def mix_out(tile):
        mine = pl.ds(pl.multiple_of(tile * TQ, TQ), TQ)
        return pltpu.make_async_copy(mix_ref.at[mine], mix_hbm.at[mine], mix_sem.at[tile])

    def dkv_out(block):
        here = pl.ds(pl.multiple_of(block * BLOCK, BLOCK), BLOCK)
        return pltpu.make_async_copy(dkv_ref.at[here], dkv_hbm.at[here], dkv_sem.at[block])

    def query_tile(tile, _):
        q_at = pl.multiple_of(tile * TQ, TQ)
        mine = pl.ds(q_at, TQ)
        qc = qc_ref[mine, :]
        qcT = qc.T
        qT, cT = qcT[:HD], qcT[HD:]
        own = [kid[(rows + q_at) // BLOCK + i] for i in range(TQ // BLOCK)]
        own = own[0] if len(own) == 1 else jnp.concatenate(own, axis=1)
        hot = jnp.where(one_hot(own), 1.0, 0.0)
        hot = jnp.concatenate([hot, jnp.zeros((HD - SAMPLES, TQ), f32)], axis=0).astype(bf16)
        q_side = jnp.concatenate([qT, hot], axis=0)
        c_side = jnp.concatenate([jnp.zeros_like(cT), cT], axis=0)
        lanes = lax.broadcasted_iota(i32, qc.shape, 1)
        q_only = jnp.where(lanes < HD, qc, jnp.zeros_like(qc))
        c_only = jnp.where(lanes < HD, jnp.zeros_like(qc), qc)
        cq = jnp.concatenate([c_only, q_only], axis=0)
        begin, end = span(rows + q_at, rows + q_at + TQ)
        first = begin // ALIGN * ALIGN
        count = (end - first + TK - 1) // TK

        def key_rows(step):
            return pl.ds(pl.multiple_of(first + step * TK, ALIGN), TK)

        def slot(step):
            return pl.ds(pl.multiple_of(step * TK, TK), TK)

        def scores_of(step):
            return jnp.dot(kaug[key_rows(step), :], q_side, preferred_element_type=f32) * log2_factor

        def bounded_step(step, total):
            terms = jnp.exp2(scores_of(step))
            pbuf[slot(step), :] = terms
            mbuf[step] = jnp.zeros((1, TQ), f32)
            return total + jnp.sum(terms, axis=0, keepdims=True)

        def running_step(step, state):
            top, total = state
            scores = scores_of(step)
            new_top = jnp.maximum(top, jnp.max(scores, axis=0, keepdims=True))
            terms = jnp.exp2(scores - new_top)
            pbuf[slot(step), :] = terms
            mbuf[step] = new_top
            return new_top, total * jnp.exp2(top - new_top) + jnp.sum(terms, axis=0, keepdims=True)

        def bounded():
            return jnp.zeros((1, TQ), f32), looped(count, bounded_step, jnp.zeros((1, TQ), f32))

        def running():
            start = (jnp.full((1, TQ), -1e30, f32), jnp.zeros((1, TQ), f32))
            return lax.fori_loop(0, count, running_step, start)

        query_most = jnp.max(squared(qT))
        small = query_most * key_most <= (SAFE_POWER / log2_factor) ** 2
        top, total = lax.cond(small, bounded, running)
        scale = 1.0 / total

        def weights_of(step):
            return pbuf[slot(step), :] * (jnp.exp2(mbuf[step] - top) * scale)

        def value_step(step, summed):
            return summed + jnp.dot(
                kvT[HD:, key_rows(step)], weights_of(step).astype(bf16), preferred_element_type=f32
            )

        mixed = looped(count, value_step, jnp.zeros((HD, TQ), f32)).astype(bf16)
        row_dot = jnp.sum(cT.astype(f32) * mixed.astype(f32), axis=0, keepdims=True)

        def grad_step(step, summed):
            keys = key_rows(step)
            weights = weights_of(step)
            grad_prob = jnp.dot(kvx[keys, :], c_side, preferred_element_type=f32)
            grad_score = (weights * (grad_prob - row_dot)).astype(bf16)
            pair = jnp.concatenate([weights.astype(bf16), grad_score], axis=1)
            acc[keys, :] += jnp.dot(pair, cq, preferred_element_type=f32)
            return summed + jnp.dot(kvT[:HD, keys], grad_score, preferred_element_type=f32)

        grad_query = looped(count, grad_step, jnp.zeros((HD, TQ), f32)) * factor
        mix_ref[mine, :] = jnp.concatenate([mixed, grad_query.astype(bf16)], axis=0).T
        mix_out(tile).start()
        return 0

    lax.fori_loop(0, rows // TQ, query_tile, 0)

    def finish(block, _):
        here = pl.ds(pl.multiple_of(block * BLOCK, BLOCK), BLOCK)
        grads = acc[here, :]
        dkv_ref[here, :] = jnp.where(lane < HD, grads * factor, grads).astype(bf16)
        dkv_out(block).start()
        return 0

    lax.fori_loop(0, ext // BLOCK, finish, 0)

    def settle_mix(tile, _):
        mix_out(tile).wait()
        return 0

    def settle_dkv(block, _):
        dkv_out(block).wait()
        return 0

    lax.fori_loop(0, rows // TQ, settle_mix, 0)
    lax.fori_loop(0, ext // BLOCK, settle_dkv, 0)


def attention(planes, qc, kv, ids):
    rows, ext = qc.shape[0], kv.shape[0]
    vmem = pl.BlockSpec(memory_space=pltpu.VMEM)
    hbm = pl.BlockSpec(memory_space=pl.ANY)
    padded = ext + max(TK, BLOCK)
    steps = (2 * rows + TQ + TK + ALIGN) // TK
    bf16, f32 = jnp.bfloat16, jnp.float32
    return pl.pallas_call(
        functools.partial(attention_kernel, planes),
        out_shape=(jax.ShapeDtypeStruct((rows, LANES), bf16),
                   jax.ShapeDtypeStruct((ext, LANES), bf16)),
        in_specs=[hbm, hbm, vmem],
        out_specs=(hbm, hbm),
        scratch_shapes=[
            pltpu.VMEM((rows, LANES), bf16),
            pltpu.VMEM((rows, LANES), bf16),
            pltpu.VMEM((ext, LANES), bf16),
            pltpu.VMEM((ext // BLOCK, 1, BLOCK), jnp.int32),
            pltpu.VMEM((padded, LANES), bf16),
            pltpu.VMEM((padded, LANES), bf16),
            pltpu.VMEM((LANES, padded), bf16),
            pltpu.VMEM((padded, LANES), f32),
            pltpu.VMEM((steps * TK, TQ), f32),
            pltpu.VMEM((steps, 1, TQ), f32),
            pltpu.SMEM((SAMPLES + 1,), jnp.int32),
            pltpu.SemaphoreType.DMA((2,)),
            pltpu.SemaphoreType.DMA((rows // TQ,)),
            pltpu.SemaphoreType.DMA((ext // BLOCK,)),
        ],
        compiler_params=pltpu.CompilerParams(vmem_limit_bytes=60 * 2**20),
        name="attention",
    )(qc, kv, ids)


def partner(me, hop, size):
    return lax.rem(me + hop, size)


def hops():
    found = []
    for start in ((1, 2), (1, 1), (0, 1), (2, 2), (0, 2)):
        turned = []
        dx, dy = start
        for _ in range(4):
            if (dx % SIDE, dy % SIDE) not in turned:
                turned.append((dx % SIDE, dy % SIDE))
            dx, dy = -dy, dx
        found += [(x, y, core) for core in range(2) for x, y in turned]
    return found + [(0, 0, 1)]


SIDE = 4
HOPS = hops()


def moved(me, hop, sign=1):
    x, y, core = me // (2 * SIDE), lax.rem(me // 2, SIDE), lax.rem(me, 2)
    dx, dy, dcore = hop
    x = lax.rem(x + (dx if sign > 0 else SIDE - dx), SIDE)
    y = lax.rem(y + (dy if sign > 0 else SIDE - dy), SIDE)
    return (x * SIDE + y) * 2 + lax.rem(core + dcore, 2)


def greet_all(me, above, below):
    barrier = pltpu.get_barrier_semaphore()
    for hop in HOPS:
        pl.semaphore_signal(barrier, inc=1, device_id={"inner": moved(me, hop)}, device_id_type=MESH)
    for other in (above, below):
        pl.semaphore_signal(barrier, inc=1, device_id={"outer": other}, device_id_type=MESH)
    return barrier, len(HOPS) + 2


def packed(first, second, head):
    columns = slice(head * HD, (head + 1) * HD)
    return jnp.concatenate([first[:, columns], second[:, columns]], axis=1)


def collect_kernel(size, planes, q_hbm, k_hbm, v_hbm, c_hbm, id_ref, qc_ref, kv_ref, ids_ref,
                   q_ref, k_ref, v_ref, c_ref, qc_pack, kv_pack, in_sem, own_sem, kv_send, kv_recv, qc_send, qc_recv,
                   id_send, id_recv, z_send, z_recv, zid_send, zid_recv):
    me, plane = lax.axis_index("inner"), lax.axis_index("outer")
    tok = q_ref.shape[0]
    rows = tok * size
    above, below = partner(plane, 1, planes), partner(plane, planes - 1, planes)
    loads = [
        pltpu.make_async_copy(source, target, in_sem.at[i])
        for i, (source, target) in enumerate(((k_hbm, k_ref), (v_hbm, v_ref), (q_hbm, q_ref), (c_hbm, c_ref)))
    ]
    for load in loads:
        load.start()
    barrier, greeted = greet_all(me, above, below)
    loads[0].wait()
    loads[1].wait()
    for head in range(size):
        kv_pack[head] = packed(k_ref, v_ref, head)
    pl.semaphore_wait(barrier, greeted)

    def block(owner, base=0):
        return pl.ds(pl.multiple_of(base + owner * tok, tok), tok)

    def kv_copy(other, slot):
        return pltpu.make_async_remote_copy(
            src_ref=kv_pack.at[other], dst_ref=kv_ref.at[block(slot, rows)],
            send_sem=kv_send.at[other], recv_sem=kv_recv.at[slot],
            device_id={"inner": other}, device_id_type=MESH)

    def qc_copy(other, slot):
        return pltpu.make_async_remote_copy(
            src_ref=qc_pack.at[other], dst_ref=qc_ref.at[block(slot)],
            send_sem=qc_send.at[other], recv_sem=qc_recv.at[slot],
            device_id={"inner": other}, device_id_type=MESH)

    def id_copy(other, slot):
        return pltpu.make_async_remote_copy(
            src_ref=id_ref, dst_ref=ids_ref.at[1, pl.ds(slot, 1)],
            send_sem=id_send.at[other], recv_sem=id_recv.at[slot],
            device_id={"inner": other}, device_id_type=MESH)

    def z_copies(slot):
        src = kv_ref.at[block(slot, rows)]
        up = pltpu.make_async_remote_copy(
            src_ref=src, dst_ref=kv_ref.at[block(slot)],
            send_sem=z_send.at[0, slot], recv_sem=z_recv.at[0, slot],
            device_id={"outer": above}, device_id_type=MESH)
        down = pltpu.make_async_remote_copy(
            src_ref=src, dst_ref=kv_ref.at[block(slot, 2 * rows)],
            send_sem=z_send.at[1, slot], recv_sem=z_recv.at[1, slot],
            device_id={"outer": below}, device_id_type=MESH)
        return up, down

    own_kv = pltpu.make_async_copy(kv_pack.at[me], kv_ref.at[block(me, rows)], own_sem.at[0])
    own_id = pltpu.make_async_copy(id_ref, ids_ref.at[1, pl.ds(me, 1)], own_sem.at[1])
    own_kv.start()
    own_id.start()
    for hop in HOPS:
        other = moved(me, hop)
        kv_copy(other, me).start()
        id_copy(other, me).start()
    own_kv.wait()
    for copy in z_copies(me):
        copy.start()
    loads[2].wait()
    loads[3].wait()
    for head in range(size):
        qc_pack[head] = packed(q_ref, c_ref, head)
    own_qc = pltpu.make_async_copy(qc_pack.at[me], qc_ref.at[block(me)], own_sem.at[2])
    own_qc.start()
    for hop in HOPS:
        qc_copy(moved(me, hop), me).start()
    for hop in HOPS:
        slot = moved(me, hop, -1)
        kv_copy(slot, slot).wait_recv()
        for copy in z_copies(slot):
            copy.start()
    own_id.wait()
    for hop in HOPS:
        slot = moved(me, hop, -1)
        id_copy(slot, slot).wait_recv()
    id_up = pltpu.make_async_remote_copy(
        src_ref=ids_ref.at[1], dst_ref=ids_ref.at[0], send_sem=zid_send.at[0], recv_sem=zid_recv.at[0],
        device_id={"outer": above}, device_id_type=MESH)
    id_down = pltpu.make_async_remote_copy(
        src_ref=ids_ref.at[1], dst_ref=ids_ref.at[2], send_sem=zid_send.at[1], recv_sem=zid_recv.at[1],
        device_id={"outer": below}, device_id_type=MESH)
    id_up.start()
    id_down.start()
    own_qc.wait()

    def settle(hop, _):
        slot = partner(me, hop, size)
        qc_copy(slot, slot).wait_recv()
        kv_copy(slot, me).wait_send()
        qc_copy(slot, me).wait_send()
        id_copy(slot, me).wait_send()
        return 0

    lax.fori_loop(1, size, settle, 0)
    id_up.wait()
    id_down.wait()

    def settle_z(slot, _):
        for copy in z_copies(slot):
            copy.wait()
        return 0

    lax.fori_loop(0, size, settle_z, 0)


def collect(size, planes, q, k, v, c, ids):
    tok, width = q.shape
    rows = tok * size
    vmem = pl.BlockSpec(memory_space=pltpu.VMEM)
    hbm = pl.BlockSpec(memory_space=pl.ANY)
    dma = pltpu.SemaphoreType.DMA
    return pl.pallas_call(
        functools.partial(collect_kernel, size, planes),
        out_shape=(jax.ShapeDtypeStruct((rows, LANES), jnp.bfloat16),
                   jax.ShapeDtypeStruct((3 * rows, LANES), jnp.bfloat16),
                   jax.ShapeDtypeStruct((3, size, tok), jnp.int32)),
        in_specs=[hbm] * 4 + [vmem],
        out_specs=(hbm, hbm, vmem),
        scratch_shapes=[pltpu.VMEM((tok, width), jnp.bfloat16)] * 4 + [
            pltpu.VMEM((size, tok, LANES), jnp.bfloat16),
            pltpu.VMEM((size, tok, LANES), jnp.bfloat16),
            dma((4,)), dma((3,)), dma((size,)), dma((size,)), dma((size,)), dma((size,)),
            dma((size,)), dma((size,)), dma((2, size)), dma((2, size)), dma((2,)), dma((2,)),
        ],
        compiler_params=pltpu.CompilerParams(collective_id=0, has_side_effects=True, vmem_limit_bytes=60 * 2**20),
        name="collect",
    )(q, k, v, c, ids)


def return_kernel(size, planes, mix_ref, dkv_ref, rmix_ref, rkv_ref, from_z, own, total,
                  own_sem, mix_send, mix_recv, kv_send, kv_recv, z_send, z_recv):
    me, plane = lax.axis_index("inner"), lax.axis_index("outer")
    rows = mix_ref.shape[0]
    tok = rows // size
    above, below = partner(plane, 1, planes), partner(plane, planes - 1, planes)
    own_in = pltpu.make_async_copy(dkv_ref.at[pl.ds(rows, rows)], own, own_sem.at[2])
    own_in.start()
    barrier, greeted = greet_all(me, above, below)
    pl.semaphore_wait(barrier, greeted)

    def block(owner, base=0):
        return pl.ds(pl.multiple_of(base + owner * tok, tok), tok)

    def z_copies(slot):
        down = pltpu.make_async_remote_copy(
            src_ref=dkv_ref.at[block(slot)], dst_ref=from_z.at[0, block(slot)],
            send_sem=z_send.at[0, slot], recv_sem=z_recv.at[0, slot],
            device_id={"outer": below}, device_id_type=MESH)
        up = pltpu.make_async_remote_copy(
            src_ref=dkv_ref.at[block(slot, 2 * rows)], dst_ref=from_z.at[1, block(slot)],
            send_sem=z_send.at[1, slot], recv_sem=z_recv.at[1, slot],
            device_id={"outer": above}, device_id_type=MESH)
        return down, up

    def mix_copy(other, slot):
        return pltpu.make_async_remote_copy(
            src_ref=mix_ref.at[block(other)], dst_ref=rmix_ref.at[slot],
            send_sem=mix_send.at[other], recv_sem=mix_recv.at[slot],
            device_id={"inner": other}, device_id_type=MESH)

    def kv_copy(other, slot):
        return pltpu.make_async_remote_copy(
            src_ref=total.at[block(other)], dst_ref=rkv_ref.at[slot],
            send_sem=kv_send.at[other], recv_sem=kv_recv.at[slot],
            device_id={"inner": other}, device_id_type=MESH)

    for hop in HOPS:
        other = moved(me, hop)
        for copy in z_copies(other):
            copy.start()
        mix_copy(other, me).start()
    for copy in z_copies(me):
        copy.start()
    own_mix = pltpu.make_async_copy(mix_ref.at[block(me)], rmix_ref.at[me], own_sem.at[0])
    own_mix.start()
    own_kv = pltpu.make_async_copy(total.at[block(me)], rkv_ref.at[me], own_sem.at[1])
    own_in.wait()

    def add_up(other):
        for copy in z_copies(other):
            copy.wait_recv()
        here = block(other)
        mine = own[here, :].astype(jnp.float32)
        first = from_z[0, here, :].astype(jnp.float32)
        second = from_z[1, here, :].astype(jnp.float32)
        total[here, :] = (mine + first + second).astype(jnp.bfloat16)

    for hop in HOPS:
        other = moved(me, hop)
        add_up(other)
        kv_copy(other, me).start()
    add_up(me)
    own_kv.start()
    own_mix.wait()
    own_kv.wait()

    def settle(hop, _):
        slot = partner(me, hop, size)
        mix_copy(slot, slot).wait_recv()
        kv_copy(slot, slot).wait_recv()
        mix_copy(slot, me).wait_send()
        kv_copy(slot, me).wait_send()
        return 0

    lax.fori_loop(1, size, settle, 0)

    def settle_z(slot, _):
        for copy in z_copies(slot):
            copy.wait_send()
        return 0

    lax.fori_loop(0, size, settle_z, 0)


def give_back(size, planes, mix, dkv):
    rows = mix.shape[0]
    tok = rows // size
    hbm = pl.BlockSpec(memory_space=pl.ANY)
    dma = pltpu.SemaphoreType.DMA
    got = jax.ShapeDtypeStruct((size, tok, LANES), jnp.bfloat16)
    return pl.pallas_call(
        functools.partial(return_kernel, size, planes),
        out_shape=(got, got),
        in_specs=[hbm, hbm],
        out_specs=(hbm, hbm),
        scratch_shapes=[
            pltpu.VMEM((2, rows, LANES), jnp.bfloat16),
            pltpu.VMEM((rows, LANES), jnp.bfloat16),
            pltpu.VMEM((rows, LANES), jnp.bfloat16),
            dma((3,)), dma((size,)), dma((size,)), dma((size,)), dma((size,)), dma((2, size)), dma((2, size)),
        ],
        compiler_params=pltpu.CompilerParams(collective_id=1, has_side_effects=True, vmem_limit_bytes=60 * 2**20),
        name="give_back",
    )(mix, dkv)


def unpack_kernel(rmix_ref, rkv_ref, att_ref, dq_ref, dk_ref, dv_ref):
    for head in range(rmix_ref.shape[0]):
        columns = slice(head * HD, (head + 1) * HD)
        mix, grads = rmix_ref[head], rkv_ref[head]
        att_ref[:, columns] = mix[:, :HD]
        dq_ref[:, columns] = mix[:, HD:]
        dk_ref[:, columns] = grads[:, :HD]
        dv_ref[:, columns] = grads[:, HD:]


def unpack(rmix, rkv):
    heads, tok, _ = rmix.shape
    vmem = pl.BlockSpec(memory_space=pltpu.VMEM)
    return pl.pallas_call(
        unpack_kernel,
        out_shape=(jax.ShapeDtypeStruct((tok, heads * HD), jnp.bfloat16),) * 4,
        in_specs=[vmem, vmem],
        out_specs=(vmem,) * 4,
        compiler_params=pltpu.CompilerParams(vmem_limit_bytes=32 * 2**20),
        name="unpack",
    )(rmix, rkv)


def on_device(query_rows, key_rows, value_rows, sample_of, cotangent):
    size, planes = lax.axis_size("inner"), lax.axis_size("outer")
    qc, kv, ids = collect(size, planes, query_rows, key_rows, value_rows, cotangent, sample_of[None])
    mix, dkv = attention(planes, qc, kv, ids)
    return unpack(*give_back(size, planes, mix, dkv))


def solution(mesh):
    rows = P(("outer", "inner"), None)
    return jax.shard_map(
        on_device, mesh=mesh,
        in_specs=(rows, rows, rows, P(("outer", "inner")), rows),
        out_specs=(rows,) * 4, check_vma=False,
    )
```

```python
import functools, math
import jax, jax.numpy as jnp
from jax import lax
from jax.sharding import PartitionSpec as P
from jax.experimental import pallas as pl
from jax.experimental.pallas import tpu as pltpu

HD, SAMPLES = 64, 8
LANES = 2 * HD
MESH = pl.DeviceIdType.MESH
TQ, TK, BLOCK, ALIGN = 512, 256, 512, 128
LEVELS = (8, 2, 1)
PENALTY = -float(2**20)
SAFE_POWER = 100.0


def looped(count, step, state, levels=None):
    done = 0
    for level in levels or LEVELS:

        def several(turn, state, level=level, done=done):
            for i in range(level):
                state = step(done + turn * level + i, state)
            return state

        turns = (count - done) // level
        state = lax.fori_loop(0, turns, several, state)
        done = done + turns * level
    return state


def attention_kernel(planes, qc_hbm, kv_hbm, ids_ref, mix_hbm, dkv_hbm,
                     qc_ref, kid, kaug, kvx, kvT, acc, pbuf, mbuf, edges,
                     in_sem, mix_sem, dkv_sem):
    f32, bf16, i32 = jnp.float32, jnp.bfloat16, jnp.int32
    rows, ext = qc_hbm.shape[0], kv_hbm.shape[0]
    kv_in = pltpu.make_async_copy(kv_hbm, kvx.at[pl.ds(0, ext)], in_sem.at[0])
    qc_in = pltpu.make_async_copy(qc_hbm, qc_ref, in_sem.at[1])
    kv_in.start()
    qc_in.start()
    _, owners, tok = ids_ref.shape
    per_block = BLOCK // tok
    factor = 1.0 / math.sqrt(HD)
    log2_factor = factor * math.log2(math.e)
    plane = lax.axis_index("outer")

    before = jnp.where(plane == 0, -1, ids_ref[0])
    after = jnp.where(plane == planes - 1, SAMPLES, ids_ref[2])
    parts = (before, ids_ref[1], after)
    for sample in range(SAMPLES + 1):
        low = sum((part < sample).astype(i32) for part in parts)
        edges[sample] = jnp.sum(low)
    for place, part in enumerate(parts):
        for owner in range(owners):
            at = place * owners + owner
            kid[at // per_block, :, (at % per_block) * tok:(at % per_block + 1) * tok] = part[owner:owner + 1]

    def span(begin, end):
        first, last = edges[0] * 0, edges[0] * 0 + ext
        for sample in range(SAMPLES + 1):
            edge = edges[sample]
            first = jnp.where(edge <= begin, jnp.maximum(first, edge), first)
            last = jnp.where(edge >= end, jnp.minimum(last, edge), last)
        return first, last

    def one_hot(ids_row):
        width = ids_row.shape[1]
        sample = lax.broadcasted_iota(i32, (SAMPLES, width), 0)
        return sample == jnp.broadcast_to(ids_row, (SAMPLES, width))

    lane = lax.broadcasted_iota(i32, (BLOCK, LANES), 1)

    def clear(block, _):
        acc[pl.ds(pl.multiple_of(block * BLOCK, BLOCK), BLOCK), :] = jnp.zeros((BLOCK, LANES), f32)
        return 0

    looped(acc.shape[0] // BLOCK, clear, 0, (5, 1))

    def squared(turned):
        wide = turned.astype(f32)
        return jnp.sum(wide * wide, axis=0, keepdims=True)

    def prepare(block, largest):
        here = pl.ds(pl.multiple_of(block * BLOCK, BLOCK), BLOCK)
        turned = kvx[here, :].T
        kvT[:, here] = turned
        penalty = jnp.where(one_hot(kid[block]), 0.0, PENALTY)
        penalty = jnp.concatenate([penalty, jnp.zeros((HD - SAMPLES, BLOCK), f32)], axis=0)
        kaug[here, :] = jnp.concatenate([turned[:HD], penalty.astype(bf16)], axis=0).T
        return jnp.maximum(largest, squared(turned[:HD]))

    kv_in.wait()
    reach_first, reach_last = span(rows, 2 * rows)
    first_block = reach_first // BLOCK
    last_block = (reach_last + BLOCK - 1) // BLOCK
    key_square = looped(
        last_block - first_block, lambda i, largest: prepare(first_block + i, largest), jnp.zeros((1, BLOCK), f32), (4, 1)
    )
    key_most = jnp.max(key_square)

    def pad(block):
        here = pl.ds(pl.multiple_of(block * BLOCK, BLOCK), BLOCK)
        kvx[here, :] = jnp.zeros((BLOCK, LANES), bf16)
        kvT[:, here] = jnp.zeros((LANES, BLOCK), bf16)
        kaug[here, :] = jnp.where((lane >= HD) & (lane < HD + SAMPLES), PENALTY, 0.0).astype(bf16)

    pad(last_block)
    qc_in.wait()

    def mix_out(tile):
        mine = pl.ds(pl.multiple_of(tile * TQ, TQ), TQ)
        return pltpu.make_async_copy(qc_ref.at[mine], mix_hbm.at[mine], mix_sem.at[tile])

    def dkv_out(block):
        here = pl.ds(pl.multiple_of(block * BLOCK, BLOCK), BLOCK)
        return pltpu.make_async_copy(kvx.at[here], dkv_hbm.at[here], dkv_sem.at[block])

    def query_tile(tile, _):
        q_at = pl.multiple_of(tile * TQ, TQ)
        mine = pl.ds(q_at, TQ)
        qc = qc_ref[mine, :]
        qcT = qc.T
        qT, cT = qcT[:HD], qcT[HD:]
        own = [kid[(rows + q_at) // BLOCK + i] for i in range(TQ // BLOCK)]
        own = own[0] if len(own) == 1 else jnp.concatenate(own, axis=1)
        hot = jnp.where(one_hot(own), 1.0, 0.0)
        hot = jnp.concatenate([hot, jnp.zeros((HD - SAMPLES, TQ), f32)], axis=0).astype(bf16)
        q_side = jnp.concatenate([qT, hot], axis=0)
        c_side = jnp.concatenate([jnp.zeros_like(cT), cT], axis=0)
        lanes = lax.broadcasted_iota(i32, qc.shape, 1)
        q_only = jnp.where(lanes < HD, qc, jnp.zeros_like(qc))
        c_only = jnp.where(lanes < HD, jnp.zeros_like(qc), qc)
        cq = jnp.concatenate([c_only, q_only], axis=0)
        begin, end = span(rows + q_at, rows + q_at + TQ)
        first = begin // ALIGN * ALIGN
        count = (end - first + TK - 1) // TK

        def key_rows(step):
            return pl.ds(pl.multiple_of(first + step * TK, ALIGN), TK)

        def slot(step):
            return pl.ds(pl.multiple_of(step * TK, TK), TK)

        def scores_of(step):
            return jnp.dot(kaug[key_rows(step), :], q_side, preferred_element_type=f32) * log2_factor

        def bounded_step(step, total):
            terms = jnp.exp2(scores_of(step))
            pbuf[slot(step), :] = terms
            mbuf[step] = jnp.zeros((1, TQ), f32)
            return total + jnp.sum(terms, axis=0, keepdims=True)

        def running_step(step, state):
            top, total = state
            scores = scores_of(step)
            new_top = jnp.maximum(top, jnp.max(scores, axis=0, keepdims=True))
            terms = jnp.exp2(scores - new_top)
            pbuf[slot(step), :] = terms
            mbuf[step] = new_top
            return new_top, total * jnp.exp2(top - new_top) + jnp.sum(terms, axis=0, keepdims=True)

        def bounded():
            return jnp.zeros((1, TQ), f32), looped(count, bounded_step, jnp.zeros((1, TQ), f32))

        def running():
            start = (jnp.full((1, TQ), -1e30, f32), jnp.zeros((1, TQ), f32))
            return lax.fori_loop(0, count, running_step, start)

        query_most = jnp.max(squared(qT))
        small = query_most * key_most <= (SAFE_POWER / log2_factor) ** 2
        top, total = lax.cond(small, bounded, running)
        scale = 1.0 / total

        def weights_of(step):
            return pbuf[slot(step), :] * (jnp.exp2(mbuf[step] - top) * scale)

        def value_step(step, summed):
            return summed + jnp.dot(
                kvT[HD:, key_rows(step)], weights_of(step).astype(bf16), preferred_element_type=f32
            )

        mixed = looped(count, value_step, jnp.zeros((HD, TQ), f32)).astype(bf16)
        row_dot = jnp.sum(cT.astype(f32) * mixed.astype(f32), axis=0, keepdims=True)

        def grad_step(step, summed):
            keys = key_rows(step)
            weights = weights_of(step)
            grad_prob = jnp.dot(kvx[keys, :], c_side, preferred_element_type=f32)
            grad_score = (weights * (grad_prob - row_dot)).astype(bf16)
            pair = jnp.concatenate([weights.astype(bf16), grad_score], axis=1)
            acc[keys, :] += jnp.dot(pair, cq, preferred_element_type=f32)
            return summed + jnp.dot(kvT[:HD, keys], grad_score, preferred_element_type=f32)

        grad_query = looped(count, grad_step, jnp.zeros((HD, TQ), f32)) * factor
        qc_ref[mine, :] = jnp.concatenate([mixed, grad_query.astype(bf16)], axis=0).T
        mix_out(tile).start()
        return 0

    lax.fori_loop(0, rows // TQ, query_tile, 0)

    def finish(block, _):
        here = pl.ds(pl.multiple_of(block * BLOCK, BLOCK), BLOCK)
        grads = acc[here, :]
        kvx[here, :] = jnp.where(lane < HD, grads * factor, grads).astype(bf16)
        dkv_out(block).start()
        return 0

    looped(ext // BLOCK, finish, 0, (4, 1))

    def settle_mix(tile, _):
        mix_out(tile).wait()
        return 0

    def settle_dkv(block, _):
        dkv_out(block).wait()
        return 0

    lax.fori_loop(0, rows // TQ, settle_mix, 0)
    lax.fori_loop(0, ext // BLOCK, settle_dkv, 0)


def attention(planes, qc, kv, ids):
    rows, ext = qc.shape[0], kv.shape[0]
    vmem = pl.BlockSpec(memory_space=pltpu.VMEM)
    hbm = pl.BlockSpec(memory_space=pl.ANY)
    padded = ext + max(TK, BLOCK)
    steps = (2 * rows + TQ + TK + ALIGN) // TK
    bf16, f32 = jnp.bfloat16, jnp.float32
    return pl.pallas_call(
        functools.partial(attention_kernel, planes),
        out_shape=(jax.ShapeDtypeStruct((rows, LANES), bf16),
                   jax.ShapeDtypeStruct((ext, LANES), bf16)),
        in_specs=[hbm, hbm, vmem],
        out_specs=(hbm, hbm),
        scratch_shapes=[
            pltpu.VMEM((rows, LANES), bf16),
            pltpu.VMEM((ext // BLOCK, 1, BLOCK), jnp.int32),
            pltpu.VMEM((padded, LANES), bf16),
            pltpu.VMEM((padded, LANES), bf16),
            pltpu.VMEM((LANES, padded), bf16),
            pltpu.VMEM((padded, LANES), f32),
            pltpu.VMEM((steps * TK, TQ), f32),
            pltpu.VMEM((steps, 1, TQ), f32),
            pltpu.SMEM((SAMPLES + 1,), jnp.int32),
            pltpu.SemaphoreType.DMA((2,)),
            pltpu.SemaphoreType.DMA((rows // TQ,)),
            pltpu.SemaphoreType.DMA((ext // BLOCK,)),
        ],
        compiler_params=pltpu.CompilerParams(vmem_limit_bytes=60 * 2**20),
        name="attention",
    )(qc, kv, ids)


def partner(me, hop, size):
    return lax.rem(me + hop, size)


def hops():
    found = []
    for start in ((1, 2), (1, 1), (0, 1), (2, 2), (0, 2)):
        turned = []
        dx, dy = start
        for _ in range(4):
            if (dx % SIDE, dy % SIDE) not in turned:
                turned.append((dx % SIDE, dy % SIDE))
            dx, dy = -dy, dx
        found += [(x, y, core) for core in range(2) for x, y in turned]
    return found + [(0, 0, 1)]


SIDE = 4
HOPS = hops()


def moved(me, hop, sign=1):
    x, y, core = me // (2 * SIDE), lax.rem(me // 2, SIDE), lax.rem(me, 2)
    dx, dy, dcore = hop
    x = lax.rem(x + (dx if sign > 0 else SIDE - dx), SIDE)
    y = lax.rem(y + (dy if sign > 0 else SIDE - dy), SIDE)
    return (x * SIDE + y) * 2 + lax.rem(core + dcore, 2)


def greet_all(me, above, below):
    barrier = pltpu.get_barrier_semaphore()
    for hop in HOPS:
        pl.semaphore_signal(barrier, inc=1, device_id={"inner": moved(me, hop)}, device_id_type=MESH)
    for other in (above, below):
        pl.semaphore_signal(barrier, inc=1, device_id={"outer": other}, device_id_type=MESH)
    return barrier, len(HOPS) + 2


def packed(first, second, head):
    columns = slice(head * HD, (head + 1) * HD)
    return jnp.concatenate([first[:, columns], second[:, columns]], axis=1)


def collect_kernel(size, planes, q_hbm, k_hbm, v_hbm, c_hbm, id_ref, qc_ref, kv_ref, ids_ref,
                   q_ref, k_ref, v_ref, c_ref, qc_pack, kv_pack, in_sem, own_sem, kv_send, kv_recv, qc_send, qc_recv,
                   id_send, id_recv, z_send, z_recv, zid_send, zid_recv):
    me, plane = lax.axis_index("inner"), lax.axis_index("outer")
    tok = q_ref.shape[0]
    rows = tok * size
    above, below = partner(plane, 1, planes), partner(plane, planes - 1, planes)
    loads = [
        pltpu.make_async_copy(source, target, in_sem.at[i])
        for i, (source, target) in enumerate(((k_hbm, k_ref), (v_hbm, v_ref), (q_hbm, q_ref), (c_hbm, c_ref)))
    ]
    for load in loads:
        load.start()
    barrier, greeted = greet_all(me, above, below)
    loads[0].wait()
    loads[1].wait()
    for head in range(size):
        kv_pack[head] = packed(k_ref, v_ref, head)
    pl.semaphore_wait(barrier, greeted)

    def block(owner, base=0):
        return pl.ds(pl.multiple_of(base + owner * tok, tok), tok)

    def kv_copy(other, slot):
        return pltpu.make_async_remote_copy(
            src_ref=kv_pack.at[other], dst_ref=kv_ref.at[block(slot, rows)],
            send_sem=kv_send.at[other], recv_sem=kv_recv.at[slot],
            device_id={"inner": other}, device_id_type=MESH)

    def qc_copy(other, slot):
        return pltpu.make_async_remote_copy(
            src_ref=qc_pack.at[other], dst_ref=qc_ref.at[block(slot)],
            send_sem=qc_send.at[other], recv_sem=qc_recv.at[slot],
            device_id={"inner": other}, device_id_type=MESH)

    def id_copy(other, slot):
        return pltpu.make_async_remote_copy(
            src_ref=id_ref, dst_ref=ids_ref.at[1, pl.ds(slot, 1)],
            send_sem=id_send.at[other], recv_sem=id_recv.at[slot],
            device_id={"inner": other}, device_id_type=MESH)

    def z_copies(slot):
        src = kv_ref.at[block(slot, rows)]
        up = pltpu.make_async_remote_copy(
            src_ref=src, dst_ref=kv_ref.at[block(slot)],
            send_sem=z_send.at[0, slot], recv_sem=z_recv.at[0, slot],
            device_id={"outer": above}, device_id_type=MESH)
        down = pltpu.make_async_remote_copy(
            src_ref=src, dst_ref=kv_ref.at[block(slot, 2 * rows)],
            send_sem=z_send.at[1, slot], recv_sem=z_recv.at[1, slot],
            device_id={"outer": below}, device_id_type=MESH)
        return up, down

    own_kv = pltpu.make_async_copy(kv_pack.at[me], kv_ref.at[block(me, rows)], own_sem.at[0])
    own_id = pltpu.make_async_copy(id_ref, ids_ref.at[1, pl.ds(me, 1)], own_sem.at[1])
    own_kv.start()
    own_id.start()
    for hop in HOPS:
        other = moved(me, hop)
        kv_copy(other, me).start()
        id_copy(other, me).start()
    own_kv.wait()
    for copy in z_copies(me):
        copy.start()
    loads[2].wait()
    loads[3].wait()
    for head in range(size):
        qc_pack[head] = packed(q_ref, c_ref, head)
    own_qc = pltpu.make_async_copy(qc_pack.at[me], qc_ref.at[block(me)], own_sem.at[2])
    own_qc.start()
    for hop in HOPS:
        qc_copy(moved(me, hop), me).start()
    for hop in HOPS:
        slot = moved(me, hop, -1)
        kv_copy(slot, slot).wait_recv()
        for copy in z_copies(slot):
            copy.start()
    own_id.wait()
    for hop in HOPS:
        slot = moved(me, hop, -1)
        id_copy(slot, slot).wait_recv()
    id_up = pltpu.make_async_remote_copy(
        src_ref=ids_ref.at[1], dst_ref=ids_ref.at[0], send_sem=zid_send.at[0], recv_sem=zid_recv.at[0],
        device_id={"outer": above}, device_id_type=MESH)
    id_down = pltpu.make_async_remote_copy(
        src_ref=ids_ref.at[1], dst_ref=ids_ref.at[2], send_sem=zid_send.at[1], recv_sem=zid_recv.at[1],
        device_id={"outer": below}, device_id_type=MESH)
    id_up.start()
    id_down.start()
    own_qc.wait()

    def settle(hop, _):
        slot = partner(me, hop, size)
        qc_copy(slot, slot).wait_recv()
        kv_copy(slot, me).wait_send()
        qc_copy(slot, me).wait_send()
        id_copy(slot, me).wait_send()
        return 0

    lax.fori_loop(1, size, settle, 0)
    id_up.wait()
    id_down.wait()

    def settle_z(slot, _):
        for copy in z_copies(slot):
            copy.wait()
        return 0

    lax.fori_loop(0, size, settle_z, 0)


def collect(size, planes, q, k, v, c, ids):
    tok, width = q.shape
    rows = tok * size
    vmem = pl.BlockSpec(memory_space=pltpu.VMEM)
    hbm = pl.BlockSpec(memory_space=pl.ANY)
    dma = pltpu.SemaphoreType.DMA
    return pl.pallas_call(
        functools.partial(collect_kernel, size, planes),
        out_shape=(jax.ShapeDtypeStruct((rows, LANES), jnp.bfloat16),
                   jax.ShapeDtypeStruct((3 * rows, LANES), jnp.bfloat16),
                   jax.ShapeDtypeStruct((3, size, tok), jnp.int32)),
        in_specs=[hbm] * 4 + [vmem],
        out_specs=(hbm, hbm, vmem),
        scratch_shapes=[pltpu.VMEM((tok, width), jnp.bfloat16)] * 4 + [
            pltpu.VMEM((size, tok, LANES), jnp.bfloat16),
            pltpu.VMEM((size, tok, LANES), jnp.bfloat16),
            dma((4,)), dma((3,)), dma((size,)), dma((size,)), dma((size,)), dma((size,)),
            dma((size,)), dma((size,)), dma((2, size)), dma((2, size)), dma((2,)), dma((2,)),
        ],
        compiler_params=pltpu.CompilerParams(collective_id=0, has_side_effects=True, vmem_limit_bytes=60 * 2**20),
        name="collect",
    )(q, k, v, c, ids)


def return_kernel(size, planes, mix_ref, dkv_ref, rmix_ref, rkv_ref, from_z, own, total,
                  own_sem, mix_send, mix_recv, kv_send, kv_recv, z_send, z_recv):
    me, plane = lax.axis_index("inner"), lax.axis_index("outer")
    rows = mix_ref.shape[0]
    tok = rows // size
    above, below = partner(plane, 1, planes), partner(plane, planes - 1, planes)
    own_in = pltpu.make_async_copy(dkv_ref.at[pl.ds(rows, rows)], own, own_sem.at[2])
    own_in.start()
    barrier, greeted = greet_all(me, above, below)
    pl.semaphore_wait(barrier, greeted)

    def block(owner, base=0):
        return pl.ds(pl.multiple_of(base + owner * tok, tok), tok)

    def z_copies(slot):
        down = pltpu.make_async_remote_copy(
            src_ref=dkv_ref.at[block(slot)], dst_ref=from_z.at[0, block(slot)],
            send_sem=z_send.at[0, slot], recv_sem=z_recv.at[0, slot],
            device_id={"outer": below}, device_id_type=MESH)
        up = pltpu.make_async_remote_copy(
            src_ref=dkv_ref.at[block(slot, 2 * rows)], dst_ref=from_z.at[1, block(slot)],
            send_sem=z_send.at[1, slot], recv_sem=z_recv.at[1, slot],
            device_id={"outer": above}, device_id_type=MESH)
        return down, up

    def mix_copy(other, slot):
        return pltpu.make_async_remote_copy(
            src_ref=mix_ref.at[block(other)], dst_ref=rmix_ref.at[slot],
            send_sem=mix_send.at[other], recv_sem=mix_recv.at[slot],
            device_id={"inner": other}, device_id_type=MESH)

    def kv_copy(other, slot):
        return pltpu.make_async_remote_copy(
            src_ref=total.at[block(other)], dst_ref=rkv_ref.at[slot],
            send_sem=kv_send.at[other], recv_sem=kv_recv.at[slot],
            device_id={"inner": other}, device_id_type=MESH)

    for hop in HOPS:
        other = moved(me, hop)
        for copy in z_copies(other):
            copy.start()
        mix_copy(other, me).start()
    for copy in z_copies(me):
        copy.start()
    own_mix = pltpu.make_async_copy(mix_ref.at[block(me)], rmix_ref.at[me], own_sem.at[0])
    own_mix.start()
    own_kv = pltpu.make_async_copy(total.at[block(me)], rkv_ref.at[me], own_sem.at[1])
    own_in.wait()

    def add_up(other):
        for copy in z_copies(other):
            copy.wait_recv()
        here = block(other)
        mine = own[here, :].astype(jnp.float32)
        first = from_z[0, here, :].astype(jnp.float32)
        second = from_z[1, here, :].astype(jnp.float32)
        total[here, :] = (mine + first + second).astype(jnp.bfloat16)

    for hop in HOPS:
        other = moved(me, hop)
        add_up(other)
        kv_copy(other, me).start()
    add_up(me)
    own_kv.start()
    own_mix.wait()
    own_kv.wait()

    def settle(hop, _):
        slot = partner(me, hop, size)
        mix_copy(slot, slot).wait_recv()
        kv_copy(slot, slot).wait_recv()
        mix_copy(slot, me).wait_send()
        kv_copy(slot, me).wait_send()
        return 0

    lax.fori_loop(1, size, settle, 0)

    def settle_z(slot, _):
        for copy in z_copies(slot):
            copy.wait_send()
        return 0

    lax.fori_loop(0, size, settle_z, 0)


def give_back(size, planes, mix, dkv):
    rows = mix.shape[0]
    tok = rows // size
    hbm = pl.BlockSpec(memory_space=pl.ANY)
    dma = pltpu.SemaphoreType.DMA
    got = jax.ShapeDtypeStruct((size, tok, LANES), jnp.bfloat16)
    return pl.pallas_call(
        functools.partial(return_kernel, size, planes),
        out_shape=(got, got),
        in_specs=[hbm, hbm],
        out_specs=(hbm, hbm),
        scratch_shapes=[
            pltpu.VMEM((2, rows, LANES), jnp.bfloat16),
            pltpu.VMEM((rows, LANES), jnp.bfloat16),
            pltpu.VMEM((rows, LANES), jnp.bfloat16),
            dma((3,)), dma((size,)), dma((size,)), dma((size,)), dma((size,)), dma((2, size)), dma((2, size)),
        ],
        compiler_params=pltpu.CompilerParams(collective_id=1, has_side_effects=True, vmem_limit_bytes=60 * 2**20),
        name="give_back",
    )(mix, dkv)


def unpack_kernel(rmix_hbm, rkv_hbm, att_hbm, dq_hbm, dk_hbm, dv_hbm, rmix, rkv, att, dq, dk, dv, in_sem, out_sem):
    heads = rmix.shape[0]
    groups = in_sem.shape[1]
    each = heads // groups
    outs = ((att, att_hbm), (dq, dq_hbm), (dk, dk_hbm), (dv, dv_hbm))

    def loads(group):
        part = slice(group * each, (group + 1) * each)
        return [
            pltpu.make_async_copy(source.at[part], target.at[part], in_sem.at[i, group])
            for i, (source, target) in enumerate(((rmix_hbm, rmix), (rkv_hbm, rkv)))
        ]

    def stores(group):
        columns = slice(group * each * HD, (group + 1) * each * HD)
        return [
            pltpu.make_async_copy(source.at[:, columns], target.at[:, columns], out_sem.at[i, group])
            for i, (source, target) in enumerate(outs)
        ]

    for group in range(groups):
        for copy in loads(group):
            copy.start()
    for group in range(groups):
        for copy in loads(group):
            copy.wait()
        for head in range(group * each, (group + 1) * each):
            columns = slice(head * HD, (head + 1) * HD)
            mix, grads = rmix[head], rkv[head]
            att[:, columns] = mix[:, :HD]
            dq[:, columns] = mix[:, HD:]
            dk[:, columns] = grads[:, :HD]
            dv[:, columns] = grads[:, HD:]
        for copy in stores(group):
            copy.start()
    for group in range(groups):
        for copy in stores(group):
            copy.wait()


def unpack(rmix, rkv):
    heads, tok, _ = rmix.shape
    groups = 4
    hbm = pl.BlockSpec(memory_space=pl.ANY)
    rows = (tok, heads * HD)
    return pl.pallas_call(
        unpack_kernel,
        out_shape=(jax.ShapeDtypeStruct(rows, jnp.bfloat16),) * 4,
        in_specs=[hbm, hbm],
        out_specs=(hbm,) * 4,
        scratch_shapes=[pltpu.VMEM(rmix.shape, jnp.bfloat16)] * 2 + [pltpu.VMEM(rows, jnp.bfloat16)] * 4 + [
            pltpu.SemaphoreType.DMA((2, groups)), pltpu.SemaphoreType.DMA((4, groups))],
        compiler_params=pltpu.CompilerParams(vmem_limit_bytes=60 * 2**20),
        name="unpack",
    )(rmix, rkv)


def on_device(query_rows, key_rows, value_rows, sample_of, cotangent):
    size, planes = lax.axis_size("inner"), lax.axis_size("outer")
    qc, kv, ids = collect(size, planes, query_rows, key_rows, value_rows, cotangent, sample_of[None])
    mix, dkv = attention(planes, qc, kv, ids)
    return unpack(*give_back(size, planes, mix, dkv))


def solution(mesh):
    rows = P(("outer", "inner"), None)
    return jax.shard_map(
        on_device, mesh=mesh,
        in_specs=(rows, rows, rows, P(("outer", "inner")), rows),
        out_specs=(rows,) * 4, check_vma=False,
    )
```

```python
import functools, math
import jax, jax.numpy as jnp
from jax import lax
from jax.sharding import PartitionSpec as P
from jax.experimental import pallas as pl
from jax.experimental.pallas import tpu as pltpu

HD, SAMPLES = 64, 8
LANES = 2 * HD
MESH = pl.DeviceIdType.MESH
TQ, TK, BLOCK, ALIGN = 512, 256, 512, 128
LEVELS = (8, 2, 1)
PART = 8
PENALTY = -float(2**20)
SAFE_POWER = 100.0


def looped(count, step, state, levels=None):
    done = 0
    for level in levels or LEVELS:

        def several(turn, state, level=level, done=done):
            for i in range(level):
                state = step(done + turn * level + i, state)
            return state

        turns = (count - done) // level
        state = lax.fori_loop(0, turns, several, state)
        done = done + turns * level
    return state


def attention_kernel(planes, qc_hbm, kv_hbm, ids_ref, mix_hbm, dkv_hbm,
                     qc_ref, kid, kaug, kvx, kvT, acc, pbuf, mbuf, edges,
                     in_sem, mix_sem, dkv_sem):
    f32, bf16, i32 = jnp.float32, jnp.bfloat16, jnp.int32
    rows, ext = qc_hbm.shape[0], kv_hbm.shape[0]
    kv_in = pltpu.make_async_copy(kv_hbm, kvx.at[pl.ds(0, ext)], in_sem.at[0])
    qc_in = pltpu.make_async_copy(qc_hbm, qc_ref, in_sem.at[1])
    kv_in.start()
    qc_in.start()
    _, owners, tok = ids_ref.shape
    per_block = BLOCK // tok
    factor = 1.0 / math.sqrt(HD)
    log2_factor = factor * math.log2(math.e)
    plane = lax.axis_index("outer")

    before = jnp.where(plane == 0, -1, ids_ref[0])
    after = jnp.where(plane == planes - 1, SAMPLES, ids_ref[2])
    parts = (before, ids_ref[1], after)
    for sample in range(SAMPLES + 1):
        low = sum((part < sample).astype(i32) for part in parts)
        edges[sample] = jnp.sum(low)
    for place, part in enumerate(parts):
        for owner in range(owners):
            at = place * owners + owner
            kid[at // per_block, :, (at % per_block) * tok:(at % per_block + 1) * tok] = part[owner:owner + 1]

    def span(begin, end):
        first, last = edges[0] * 0, edges[0] * 0 + ext
        for sample in range(SAMPLES + 1):
            edge = edges[sample]
            first = jnp.where(edge <= begin, jnp.maximum(first, edge), first)
            last = jnp.where(edge >= end, jnp.minimum(last, edge), last)
        return first, last

    def one_hot(ids_row):
        width = ids_row.shape[1]
        sample = lax.broadcasted_iota(i32, (SAMPLES, width), 0)
        return sample == jnp.broadcast_to(ids_row, (SAMPLES, width))

    lane = lax.broadcasted_iota(i32, (BLOCK, LANES), 1)

    def clear(block, _):
        acc[pl.ds(pl.multiple_of(block * BLOCK, BLOCK), BLOCK), :] = jnp.zeros((BLOCK, LANES), f32)
        return 0

    looped(acc.shape[0] // BLOCK, clear, 0, (5, 1))

    def squared(turned):
        wide = turned.astype(f32)
        return jnp.sum(wide * wide, axis=0, keepdims=True)

    def prepare(block, largest):
        here = pl.ds(pl.multiple_of(block * BLOCK, BLOCK), BLOCK)
        turned = kvx[here, :].T
        kvT[:, here] = turned
        penalty = jnp.where(one_hot(kid[block]), 0.0, PENALTY)
        penalty = jnp.concatenate([penalty, jnp.zeros((HD - SAMPLES, BLOCK), f32)], axis=0)
        kaug[here, :] = jnp.concatenate([turned[:HD], penalty.astype(bf16)], axis=0).T
        return jnp.maximum(largest, squared(turned[:HD]))

    kv_in.wait()
    reach_first, reach_last = span(rows, 2 * rows)
    first_block = reach_first // BLOCK
    last_block = (reach_last + BLOCK - 1) // BLOCK
    key_square = looped(
        last_block - first_block, lambda i, largest: prepare(first_block + i, largest), jnp.zeros((1, BLOCK), f32), (4, 1)
    )
    key_most = jnp.max(key_square)

    def pad(block):
        here = pl.ds(pl.multiple_of(block * BLOCK, BLOCK), BLOCK)
        kvx[here, :] = jnp.zeros((BLOCK, LANES), bf16)
        kvT[:, here] = jnp.zeros((LANES, BLOCK), bf16)
        kaug[here, :] = jnp.where((lane >= HD) & (lane < HD + SAMPLES), PENALTY, 0.0).astype(bf16)

    pad(last_block)
    qc_in.wait()

    def mix_out(tile):
        mine = pl.ds(pl.multiple_of(tile * TQ, TQ), TQ)
        return pltpu.make_async_copy(qc_ref.at[mine], mix_hbm.at[mine], mix_sem.at[tile])

    def dkv_out(block):
        here = pl.ds(pl.multiple_of(block * BLOCK, BLOCK), BLOCK)
        return pltpu.make_async_copy(kvx.at[here], dkv_hbm.at[here], dkv_sem.at[block])

    def query_tile(tile, _):
        q_at = pl.multiple_of(tile * TQ, TQ)
        mine = pl.ds(q_at, TQ)
        qc = qc_ref[mine, :]
        qcT = qc.T
        qT, cT = qcT[:HD], qcT[HD:]
        own = [kid[(rows + q_at) // BLOCK + i] for i in range(TQ // BLOCK)]
        own = own[0] if len(own) == 1 else jnp.concatenate(own, axis=1)
        hot = jnp.where(one_hot(own), 1.0, 0.0)
        hot = jnp.concatenate([hot, jnp.zeros((HD - SAMPLES, TQ), f32)], axis=0).astype(bf16)
        q_side = jnp.concatenate([qT, hot], axis=0)
        c_side = jnp.concatenate([jnp.zeros_like(cT), cT], axis=0)
        lanes = lax.broadcasted_iota(i32, qc.shape, 1)
        q_only = jnp.where(lanes < HD, qc, jnp.zeros_like(qc))
        c_only = jnp.where(lanes < HD, jnp.zeros_like(qc), qc)
        cq = jnp.concatenate([c_only, q_only], axis=0)
        begin, end = span(rows + q_at, rows + q_at + TQ)
        first = begin // ALIGN * ALIGN
        count = (end - first + TK - 1) // TK

        def key_rows(step):
            return pl.ds(pl.multiple_of(first + step * TK, ALIGN), TK)

        def slot(step):
            return pl.ds(pl.multiple_of(step * TK, TK), TK)

        def scores_of(step):
            return jnp.dot(kaug[key_rows(step), :], q_side, preferred_element_type=f32) * log2_factor

        def bounded_step(step, total):
            terms = jnp.exp2(scores_of(step))
            pbuf[slot(step), :] = terms
            mbuf[step] = jnp.zeros((1, TQ), f32)
            return total + jnp.sum(terms.reshape(TK // PART, PART, TQ), axis=0)

        def running_step(step, state):
            top, total = state
            scores = scores_of(step)
            new_top = jnp.maximum(top, jnp.max(scores, axis=0, keepdims=True))
            terms = jnp.exp2(scores - new_top)
            pbuf[slot(step), :] = terms
            mbuf[step] = new_top
            return new_top, total * jnp.exp2(top - new_top) + jnp.sum(terms, axis=0, keepdims=True)

        def bounded():
            return jnp.zeros((1, TQ), f32), jnp.sum(looped(count, bounded_step, jnp.zeros((PART, TQ), f32), LEVELS), axis=0, keepdims=True)

        def running():
            start = (jnp.full((1, TQ), -1e30, f32), jnp.zeros((1, TQ), f32))
            return lax.fori_loop(0, count, running_step, start)

        query_most = jnp.max(squared(qT))
        small = query_most * key_most <= (SAFE_POWER / log2_factor) ** 2
        top, total = lax.cond(small, bounded, running)
        scale = 1.0 / total

        def weights_of(step):
            return pbuf[slot(step), :] * (jnp.exp2(mbuf[step] - top) * scale)

        def value_step(step, summed):
            return summed + jnp.dot(
                kvT[HD:, key_rows(step)], weights_of(step).astype(bf16), preferred_element_type=f32
            )

        mixed = looped(count, value_step, jnp.zeros((HD, TQ), f32)).astype(bf16)
        row_dot = jnp.sum(cT.astype(f32) * mixed.astype(f32), axis=0, keepdims=True)

        def grad_step(step, summed):
            keys = key_rows(step)
            weights = weights_of(step)
            grad_prob = jnp.dot(kvx[keys, :], c_side, preferred_element_type=f32)
            grad_score = (weights * (grad_prob - row_dot)).astype(bf16)
            pair = jnp.concatenate([weights.astype(bf16), grad_score], axis=1)
            acc[keys, :] += jnp.dot(pair, cq, preferred_element_type=f32)
            return summed + jnp.dot(kvT[:HD, keys], grad_score, preferred_element_type=f32)

        grad_query = looped(count, grad_step, jnp.zeros((HD, TQ), f32)) * factor
        qc_ref[mine, :] = jnp.concatenate([mixed, grad_query.astype(bf16)], axis=0).T
        mix_out(tile).start()
        return 0

    lax.fori_loop(0, rows // TQ, query_tile, 0)

    def finish(block, _):
        here = pl.ds(pl.multiple_of(block * BLOCK, BLOCK), BLOCK)
        grads = acc[here, :]
        kvx[here, :] = jnp.where(lane < HD, grads * factor, grads).astype(bf16)
        dkv_out(block).start()
        return 0

    looped(ext // BLOCK, finish, 0, (4, 1))

    def settle_mix(tile, _):
        mix_out(tile).wait()
        return 0

    def settle_dkv(block, _):
        dkv_out(block).wait()
        return 0

    lax.fori_loop(0, rows // TQ, settle_mix, 0)
    lax.fori_loop(0, ext // BLOCK, settle_dkv, 0)


def attention(planes, qc, kv, ids):
    rows, ext = qc.shape[0], kv.shape[0]
    vmem = pl.BlockSpec(memory_space=pltpu.VMEM)
    hbm = pl.BlockSpec(memory_space=pl.ANY)
    padded = ext + max(TK, BLOCK)
    steps = (2 * rows + TQ + TK + ALIGN) // TK
    bf16, f32 = jnp.bfloat16, jnp.float32
    return pl.pallas_call(
        functools.partial(attention_kernel, planes),
        out_shape=(jax.ShapeDtypeStruct((rows, LANES), bf16),
                   jax.ShapeDtypeStruct((ext, LANES), bf16)),
        in_specs=[hbm, hbm, vmem],
        out_specs=(hbm, hbm),
        scratch_shapes=[
            pltpu.VMEM((rows, LANES), bf16),
            pltpu.VMEM((ext // BLOCK, 1, BLOCK), jnp.int32),
            pltpu.VMEM((padded, LANES), bf16),
            pltpu.VMEM((padded, LANES), bf16),
            pltpu.VMEM((LANES, padded), bf16),
            pltpu.VMEM((padded, LANES), f32),
            pltpu.VMEM((steps * TK, TQ), f32),
            pltpu.VMEM((steps, 1, TQ), f32),
            pltpu.SMEM((SAMPLES + 1,), jnp.int32),
            pltpu.SemaphoreType.DMA((2,)),
            pltpu.SemaphoreType.DMA((rows // TQ,)),
            pltpu.SemaphoreType.DMA((ext // BLOCK,)),
        ],
        compiler_params=pltpu.CompilerParams(vmem_limit_bytes=60 * 2**20),
        name="attention",
    )(qc, kv, ids)


def partner(me, hop, size):
    return lax.rem(me + hop, size)


def hops():
    found = []
    for start in ((1, 2), (1, 1), (0, 1), (2, 2), (0, 2)):
        turned = []
        dx, dy = start
        for _ in range(4):
            if (dx % SIDE, dy % SIDE) not in turned:
                turned.append((dx % SIDE, dy % SIDE))
            dx, dy = -dy, dx
        found += [(x, y, core) for core in range(2) for x, y in turned]
    return found + [(0, 0, 1)]


SIDE = 4
HOPS = hops()
FIRST = HOPS[-1:] + HOPS[:-1]


def moved(me, hop, sign=1):
    x, y, core = me // (2 * SIDE), lax.rem(me // 2, SIDE), lax.rem(me, 2)
    dx, dy, dcore = hop
    x = lax.rem(x + (dx if sign > 0 else SIDE - dx), SIDE)
    y = lax.rem(y + (dy if sign > 0 else SIDE - dy), SIDE)
    return (x * SIDE + y) * 2 + lax.rem(core + dcore, 2)


def greet_all(me, above, below):
    barrier = pltpu.get_barrier_semaphore()
    for hop in HOPS:
        pl.semaphore_signal(barrier, inc=1, device_id={"inner": moved(me, hop)}, device_id_type=MESH)
    for other in (above, below):
        pl.semaphore_signal(barrier, inc=1, device_id={"outer": other}, device_id_type=MESH)
    return barrier, len(HOPS) + 2


def packed(first, second, head):
    columns = slice(head * HD, (head + 1) * HD)
    return jnp.concatenate([first[:, columns], second[:, columns]], axis=1)


def collect_kernel(size, planes, q_hbm, k_hbm, v_hbm, c_hbm, id_ref, qc_ref, kv_ref, ids_ref,
                   q_ref, k_ref, v_ref, c_ref, qc_pack, kv_pack, in_sem, own_sem, kv_send, kv_recv, qc_send, qc_recv,
                   id_send, id_recv, z_send, z_recv, zid_send, zid_recv):
    me, plane = lax.axis_index("inner"), lax.axis_index("outer")
    tok = q_ref.shape[0]
    rows = tok * size
    above, below = partner(plane, 1, planes), partner(plane, planes - 1, planes)
    loads = [
        pltpu.make_async_copy(source, target, in_sem.at[i])
        for i, (source, target) in enumerate(((k_hbm, k_ref), (v_hbm, v_ref), (q_hbm, q_ref), (c_hbm, c_ref)))
    ]
    for load in loads:
        load.start()
    barrier, greeted = greet_all(me, above, below)
    loads[0].wait()
    loads[1].wait()
    for head in range(size):
        kv_pack[head] = packed(k_ref, v_ref, head)
    pl.semaphore_wait(barrier, greeted)

    def block(owner, base=0):
        return pl.ds(pl.multiple_of(base + owner * tok, tok), tok)

    def kv_copy(other, slot):
        return pltpu.make_async_remote_copy(
            src_ref=kv_pack.at[other], dst_ref=kv_ref.at[block(slot, rows)],
            send_sem=kv_send.at[other], recv_sem=kv_recv.at[slot],
            device_id={"inner": other}, device_id_type=MESH)

    def qc_copy(other, slot):
        return pltpu.make_async_remote_copy(
            src_ref=qc_pack.at[other], dst_ref=qc_ref.at[block(slot)],
            send_sem=qc_send.at[other], recv_sem=qc_recv.at[slot],
            device_id={"inner": other}, device_id_type=MESH)

    def id_copy(other, slot):
        return pltpu.make_async_remote_copy(
            src_ref=id_ref, dst_ref=ids_ref.at[1, pl.ds(slot, 1)],
            send_sem=id_send.at[other], recv_sem=id_recv.at[slot],
            device_id={"inner": other}, device_id_type=MESH)

    def z_copies(slot, source=None):
        src = kv_ref.at[block(slot, rows)] if source is None else source
        up = pltpu.make_async_remote_copy(
            src_ref=src, dst_ref=kv_ref.at[block(slot)],
            send_sem=z_send.at[0, slot], recv_sem=z_recv.at[0, slot],
            device_id={"outer": above}, device_id_type=MESH)
        down = pltpu.make_async_remote_copy(
            src_ref=src, dst_ref=kv_ref.at[block(slot, 2 * rows)],
            send_sem=z_send.at[1, slot], recv_sem=z_recv.at[1, slot],
            device_id={"outer": below}, device_id_type=MESH)
        return up, down

    own_kv = pltpu.make_async_copy(kv_pack.at[me], kv_ref.at[block(me, rows)], own_sem.at[0])
    own_id = pltpu.make_async_copy(id_ref, ids_ref.at[1, pl.ds(me, 1)], own_sem.at[1])
    own_kv.start()
    own_id.start()
    for copy in z_copies(me, kv_pack.at[me]):
        copy.start()
    for hop in FIRST:
        kv_copy(moved(me, hop), me).start()
    for hop in FIRST:
        id_copy(moved(me, hop), me).start()
    loads[2].wait()
    loads[3].wait()
    for head in range(size):
        qc_pack[head] = packed(q_ref, c_ref, head)
    own_qc = pltpu.make_async_copy(qc_pack.at[me], qc_ref.at[block(me)], own_sem.at[2])
    own_qc.start()
    for hop in HOPS:
        qc_copy(moved(me, hop), me).start()
    for hop in FIRST:
        slot = moved(me, hop, -1)
        kv_copy(slot, slot).wait_recv()
        for copy in z_copies(slot):
            copy.start()
    own_kv.wait()
    own_id.wait()
    for hop in FIRST:
        slot = moved(me, hop, -1)
        id_copy(slot, slot).wait_recv()
    id_up = pltpu.make_async_remote_copy(
        src_ref=ids_ref.at[1], dst_ref=ids_ref.at[0], send_sem=zid_send.at[0], recv_sem=zid_recv.at[0],
        device_id={"outer": above}, device_id_type=MESH)
    id_down = pltpu.make_async_remote_copy(
        src_ref=ids_ref.at[1], dst_ref=ids_ref.at[2], send_sem=zid_send.at[1], recv_sem=zid_recv.at[1],
        device_id={"outer": below}, device_id_type=MESH)
    id_up.start()
    id_down.start()
    own_qc.wait()

    def settle(hop, _):
        slot = partner(me, hop, size)
        qc_copy(slot, slot).wait_recv()
        kv_copy(slot, me).wait_send()
        qc_copy(slot, me).wait_send()
        id_copy(slot, me).wait_send()
        return 0

    lax.fori_loop(1, size, settle, 0)
    id_up.wait()
    id_down.wait()

    def settle_z(slot, _):
        for copy in z_copies(slot):
            copy.wait()
        return 0

    lax.fori_loop(0, size, settle_z, 0)


def collect(size, planes, q, k, v, c, ids):
    tok, width = q.shape
    rows = tok * size
    vmem = pl.BlockSpec(memory_space=pltpu.VMEM)
    hbm = pl.BlockSpec(memory_space=pl.ANY)
    dma = pltpu.SemaphoreType.DMA
    return pl.pallas_call(
        functools.partial(collect_kernel, size, planes),
        out_shape=(jax.ShapeDtypeStruct((rows, LANES), jnp.bfloat16),
                   jax.ShapeDtypeStruct((3 * rows, LANES), jnp.bfloat16),
                   jax.ShapeDtypeStruct((3, size, tok), jnp.int32)),
        in_specs=[hbm] * 4 + [vmem],
        out_specs=(hbm, hbm, vmem),
        scratch_shapes=[pltpu.VMEM((tok, width), jnp.bfloat16)] * 4 + [
            pltpu.VMEM((size, tok, LANES), jnp.bfloat16),
            pltpu.VMEM((size, tok, LANES), jnp.bfloat16),
            dma((4,)), dma((3,)), dma((size,)), dma((size,)), dma((size,)), dma((size,)),
            dma((size,)), dma((size,)), dma((2, size)), dma((2, size)), dma((2,)), dma((2,)),
        ],
        compiler_params=pltpu.CompilerParams(collective_id=0, has_side_effects=True, vmem_limit_bytes=60 * 2**20),
        name="collect",
    )(q, k, v, c, ids)


def return_kernel(size, planes, mix_ref, dkv_ref, rmix_ref, rkv_ref, from_z, own, total,
                  own_sem, mix_send, mix_recv, kv_send, kv_recv, z_send, z_recv):
    me, plane = lax.axis_index("inner"), lax.axis_index("outer")
    rows = mix_ref.shape[0]
    tok = rows // size
    above, below = partner(plane, 1, planes), partner(plane, planes - 1, planes)
    own_in = pltpu.make_async_copy(dkv_ref.at[pl.ds(rows, rows)], own, own_sem.at[2])
    own_in.start()
    barrier, greeted = greet_all(me, above, below)
    pl.semaphore_wait(barrier, greeted)

    def block(owner, base=0):
        return pl.ds(pl.multiple_of(base + owner * tok, tok), tok)

    def z_copies(slot):
        down = pltpu.make_async_remote_copy(
            src_ref=dkv_ref.at[block(slot)], dst_ref=from_z.at[0, block(slot)],
            send_sem=z_send.at[0, slot], recv_sem=z_recv.at[0, slot],
            device_id={"outer": below}, device_id_type=MESH)
        up = pltpu.make_async_remote_copy(
            src_ref=dkv_ref.at[block(slot, 2 * rows)], dst_ref=from_z.at[1, block(slot)],
            send_sem=z_send.at[1, slot], recv_sem=z_recv.at[1, slot],
            device_id={"outer": above}, device_id_type=MESH)
        return down, up

    def mix_copy(other, slot):
        return pltpu.make_async_remote_copy(
            src_ref=mix_ref.at[block(other)], dst_ref=rmix_ref.at[slot],
            send_sem=mix_send.at[other], recv_sem=mix_recv.at[slot],
            device_id={"inner": other}, device_id_type=MESH)

    def kv_copy(other, slot):
        return pltpu.make_async_remote_copy(
            src_ref=total.at[block(other)], dst_ref=rkv_ref.at[slot],
            send_sem=kv_send.at[other], recv_sem=kv_recv.at[slot],
            device_id={"inner": other}, device_id_type=MESH)

    for hop in HOPS:
        other = moved(me, hop)
        for copy in z_copies(other):
            copy.start()
        mix_copy(other, me).start()
    for copy in z_copies(me):
        copy.start()
    own_mix = pltpu.make_async_copy(mix_ref.at[block(me)], rmix_ref.at[me], own_sem.at[0])
    own_mix.start()
    own_kv = pltpu.make_async_copy(total.at[block(me)], rkv_ref.at[me], own_sem.at[1])
    own_in.wait()

    def add_up(other):
        for copy in z_copies(other):
            copy.wait_recv()
        here = block(other)
        mine = own[here, :].astype(jnp.float32)
        first = from_z[0, here, :].astype(jnp.float32)
        second = from_z[1, here, :].astype(jnp.float32)
        total[here, :] = (mine + first + second).astype(jnp.bfloat16)

    for hop in HOPS:
        other = moved(me, hop)
        add_up(other)
        kv_copy(other, me).start()
    add_up(me)
    own_kv.start()
    own_mix.wait()
    own_kv.wait()

    def settle(hop, _):
        slot = partner(me, hop, size)
        mix_copy(slot, slot).wait_recv()
        kv_copy(slot, slot).wait_recv()
        mix_copy(slot, me).wait_send()
        kv_copy(slot, me).wait_send()
        return 0

    lax.fori_loop(1, size, settle, 0)

    def settle_z(slot, _):
        for copy in z_copies(slot):
            copy.wait_send()
        return 0

    lax.fori_loop(0, size, settle_z, 0)


def give_back(size, planes, mix, dkv):
    rows = mix.shape[0]
    tok = rows // size
    hbm = pl.BlockSpec(memory_space=pl.ANY)
    dma = pltpu.SemaphoreType.DMA
    got = jax.ShapeDtypeStruct((size, tok, LANES), jnp.bfloat16)
    return pl.pallas_call(
        functools.partial(return_kernel, size, planes),
        out_shape=(got, got),
        in_specs=[hbm, hbm],
        out_specs=(hbm, hbm),
        scratch_shapes=[
            pltpu.VMEM((2, rows, LANES), jnp.bfloat16),
            pltpu.VMEM((rows, LANES), jnp.bfloat16),
            pltpu.VMEM((rows, LANES), jnp.bfloat16),
            dma((3,)), dma((size,)), dma((size,)), dma((size,)), dma((size,)), dma((2, size)), dma((2, size)),
        ],
        compiler_params=pltpu.CompilerParams(collective_id=1, has_side_effects=True, vmem_limit_bytes=60 * 2**20),
        name="give_back",
    )(mix, dkv)


def unpack_kernel(rmix_hbm, rkv_hbm, att_hbm, dq_hbm, dk_hbm, dv_hbm, rmix, rkv, att, dq, dk, dv, in_sem, out_sem):
    heads = rmix.shape[0]
    groups = in_sem.shape[1]
    each = heads // groups
    outs = ((att, att_hbm), (dq, dq_hbm), (dk, dk_hbm), (dv, dv_hbm))

    def loads(group):
        part = slice(group * each, (group + 1) * each)
        return [
            pltpu.make_async_copy(source.at[part], target.at[part], in_sem.at[i, group])
            for i, (source, target) in enumerate(((rmix_hbm, rmix), (rkv_hbm, rkv)))
        ]

    def stores(group):
        columns = slice(group * each * HD, (group + 1) * each * HD)
        return [
            pltpu.make_async_copy(source.at[:, columns], target.at[:, columns], out_sem.at[i, group])
            for i, (source, target) in enumerate(outs)
        ]

    for group in range(groups):
        for copy in loads(group):
            copy.start()
    for group in range(groups):
        for copy in loads(group):
            copy.wait()
        for head in range(group * each, (group + 1) * each):
            columns = slice(head * HD, (head + 1) * HD)
            mix, grads = rmix[head], rkv[head]
            att[:, columns] = mix[:, :HD]
            dq[:, columns] = mix[:, HD:]
            dk[:, columns] = grads[:, :HD]
            dv[:, columns] = grads[:, HD:]
        for copy in stores(group):
            copy.start()
    for group in range(groups):
        for copy in stores(group):
            copy.wait()


def unpack(rmix, rkv):
    heads, tok, _ = rmix.shape
    groups = 4
    hbm = pl.BlockSpec(memory_space=pl.ANY)
    rows = (tok, heads * HD)
    return pl.pallas_call(
        unpack_kernel,
        out_shape=(jax.ShapeDtypeStruct(rows, jnp.bfloat16),) * 4,
        in_specs=[hbm, hbm],
        out_specs=(hbm,) * 4,
        scratch_shapes=[pltpu.VMEM(rmix.shape, jnp.bfloat16)] * 2 + [pltpu.VMEM(rows, jnp.bfloat16)] * 4 + [
            pltpu.SemaphoreType.DMA((2, groups)), pltpu.SemaphoreType.DMA((4, groups))],
        compiler_params=pltpu.CompilerParams(vmem_limit_bytes=60 * 2**20),
        name="unpack",
    )(rmix, rkv)


def on_device(query_rows, key_rows, value_rows, sample_of, cotangent):
    size, planes = lax.axis_size("inner"), lax.axis_size("outer")
    qc, kv, ids = collect(size, planes, query_rows, key_rows, value_rows, cotangent, sample_of[None])
    mix, dkv = attention(planes, qc, kv, ids)
    return unpack(*give_back(size, planes, mix, dkv))


def solution(mesh):
    rows = P(("outer", "inner"), None)
    return jax.shard_map(
        on_device, mesh=mesh,
        in_specs=(rows, rows, rows, P(("outer", "inner")), rows),
        out_specs=(rows,) * 4, check_vma=False,
    )
```
